512 devices in a mesh: dp: 8 (over z_lo), slab: 64 (over y, x, z_hi, core).
Axes of the slice: x: 4, y: 4, z: 16 (z_hi: 2, z_lo: 8; z = z_hi * 8 + z_lo), core: 2. Of those that a mesh axis runs over, the one named last changes fastest.
Arguments:
- features: bfloat16 [65536, 128], P(('dp', 'slab')), may hold values from -6 to 6
- counts: int32 [512], P(('dp', 'slab')), may hold values from 16 to 128, as said below
- neighbours: int32 [65536, 27], P(('dp', 'slab')), may hold values from 0 to 192, as said below
- low_faces: int32 [16384], P(('dp', 'slab')), may hold values from 0 to 127, as said below
- high_faces: int32 [16384], P(('dp', 'slab')), may hold values from 0 to 127, as said below
- weight_one: bfloat16 [27, 128, 128], replicated, may hold values from -0.109375 to 0.109375
- weight_two: bfloat16 [27, 128, 128], replicated, may hold values from -0.109375 to 0.109375
- cotangent: bfloat16 [65536, 128], P(('dp', 'slab')), may hold values from -12 to 12
Outputs:
- response: bfloat16 [65536, 128], P(('dp', 'slab'))
- input_grad: bfloat16 [65536, 128], P(('dp', 'slab'))
- first_grad: bfloat16 [27, 128, 128], replicated
- second_grad: bfloat16 [27, 128, 128], replicated
The draws below stay inside these ranges and needn't reach their ends.
Inputs may be any that keep to these rules, and one draw needn't show every extreme that they name: `counts`: at least one slab holds 128 live sites and one holds 16. `neighbours`: entry [i, 13] is i mod 128. Values below 128 name sites of the same slab, 128 to 159 the rows from the lower slab, the next 32 those from the upper slab, and 192 an empty neighbour. `low_faces`: each slab's 32 entries name its own sites, repeats allowed. `high_faces`: each slab's 32 entries name its own sites, repeats allowed.
All inputs are finite; a program needn't handle non-finite values.
Results may differ from the reference program's by a relative error of at most 0.0052.
Values may be sent and summed in bfloat16 or wider, within the bound.
No kernel may reach another device: no remote copies, remote signals or barrier semaphores. Data moves between devices by JAX's collectives and lax.ppermute only.
A program may use at most 128 MiB of HBM per device.

```python
import math
import jax
import jax.numpy as jnp
from jax import lax

SITES = 128
CHANNELS = 128
OFFSETS = 27
RIM = 32
ROWS = 65536
RIMS = 16384
N_DP = 8
N_SLAB = 64


def draw_counts(key, part):
    key = jax.random.fold_in(key, 3)
    first, second, third = jax.random.split(key, 3)
    slabs_all = ROWS // SITES
    base = jax.random.randint(first, (slabs_all,), SITES // 8, SITES // 2 + 1, dtype=jnp.int32)
    heavy = jax.random.randint(second, (slabs_all,), 0, 8, dtype=jnp.int32) == 0
    base = jnp.where(heavy, SITES, base)
    order = jax.random.permutation(third, slabs_all)
    base = base.at[order[0]].set(SITES)
    base = base.at[order[1]].set(SITES // 8)
    return base.astype(jnp.int32)


def draw_neighbours(key, part):
    key = jax.random.fold_in(key, 5)
    kinds_key, own_key, low_key, high_key = jax.random.split(key, 4)
    shape = (ROWS, OFFSETS)
    kinds = jax.random.randint(kinds_key, shape, 0, 8, dtype=jnp.int32)
    own_pick = jax.random.randint(own_key, shape, 0, SITES, dtype=jnp.int32)
    low_pick = SITES + jax.random.randint(low_key, shape, 0, RIM, dtype=jnp.int32)
    high_pick = SITES + RIM + jax.random.randint(high_key, shape, 0, RIM, dtype=jnp.int32)
    empty_pick = jnp.full(shape, SITES + 2 * RIM, jnp.int32)
    table = jnp.where(kinds < 5, own_pick, jnp.where(kinds == 5, low_pick, jnp.where(kinds == 6, high_pick, empty_pick)))
    local = (jnp.arange(ROWS, dtype=jnp.int32) % SITES).astype(jnp.int32)
    table = table.at[:, 13].set(local)
    table = table.at[:, 0].set(jnp.where(local == SITES - 1, SITES + 2 * RIM, table[:, 0]))
    return table.astype(jnp.int32)


def face_list(key):
    picks = jax.random.randint(key, (RIMS,), 0, SITES, dtype=jnp.int32)
    place = jnp.arange(RIMS, dtype=jnp.int32) % RIM
    picks = jnp.where(place == 0, 0, picks)
    picks = jnp.where(place == RIM - 1, SITES - 1, picks)
    return picks.astype(jnp.int32)


def draw_low_faces(key, part):
    key = jax.random.fold_in(key, 7)
    return face_list(key)


def draw_high_faces(key, part):
    key = jax.random.fold_in(key, 9)
    return face_list(key)


def draw_cotangent(key, part):
    key = jax.random.fold_in(key, 11)
    first = jax.random.fold_in(key, 0)
    slabs_all = ROWS // SITES
    device = (jnp.arange(ROWS, dtype=jnp.int32) // SITES).astype(jnp.float32)
    scaling = 1.0 + 2.0 * device / max(slabs_all - 1, 1)
    base = jnp.clip(jax.random.normal(first, (ROWS, CHANNELS), jnp.float32), -4.0, 4.0)
    return (base * scaling[:, None]).astype(jnp.bfloat16)


def block_levels(rng, shape, cuts, low, largest):
    gain, own = 1.0, jax.random.fold_in(rng, 6)
    for axis_at, parts in cuts:
        draws = jnp.exp(jax.random.uniform(jax.random.fold_in(own, axis_at), (parts,), jnp.float32, low / len(cuts), largest / len(cuts)))
        gain = gain * jnp.repeat(draws, shape[axis_at] // parts).reshape([-1 if axis == axis_at else 1 for axis in range(len(shape))])
    return gain


def normal_values(rng, extent, width, reach, cuts=(), kind=jnp.bfloat16):
    result = width * jax.random.normal(rng, extent, jnp.float32)
    if cuts:
        result = result * block_levels(rng, extent, cuts, -0.22, 0.18)
    return jnp.clip(result, -reach, reach).astype(kind)


def setup_inputs(seed: int = 0) -> dict:
    keys = jax.random.split(jax.random.key(seed), 9)
    features = normal_values(keys[0], (ROWS, CHANNELS), 1.0, 6.0, ((0, 512),))
    counts = draw_counts(jax.random.fold_in(keys[8], 71), 0)
    neighbours = draw_neighbours(jax.random.fold_in(keys[8], 71), 0)
    low_faces = draw_low_faces(jax.random.fold_in(keys[8], 71), 0)
    high_faces = draw_high_faces(jax.random.fold_in(keys[8], 71), 0)
    weight_one = normal_values(keys[5], (OFFSETS, CHANNELS, CHANNELS), (OFFSETS * CHANNELS) ** -0.5, 0.109375)
    weight_two = normal_values(keys[6], (OFFSETS, CHANNELS, CHANNELS), (OFFSETS * CHANNELS) ** -0.5, 0.109375)
    cotangent = draw_cotangent(jax.random.fold_in(keys[8], 71), 0)
    return dict(features=features, counts=counts, neighbours=neighbours, low_faces=low_faces, high_faces=high_faces, weight_one=weight_one, weight_two=weight_two, cotangent=cotangent)


def extend_all(values, low_faces, high_faces):
    groups = values.shape[0]
    chans = values.shape[2]
    send_up = jax.vmap(lambda v, p: v[p])(values, high_faces)
    send_down = jax.vmap(lambda v, p: v[p])(values, low_faces)
    send_up = send_up.reshape(N_DP, N_SLAB, RIM, chans)
    send_down = send_down.reshape(N_DP, N_SLAB, RIM, chans)
    zero_slab = jnp.zeros((N_DP, 1, RIM, chans), values.dtype)
    from_below = jnp.concatenate([zero_slab, send_up[:, :-1]], 1).reshape(groups, RIM, chans)
    from_above = jnp.concatenate([send_down[:, 1:], zero_slab], 1).reshape(groups, RIM, chans)
    zero_row = jnp.zeros((groups, 1, chans), values.dtype)
    return jnp.concatenate([values, from_below, from_above, zero_row], 1)

def convolve_all(extended, neighbours, weight):

    def one_slab(item):
        ext_slab, picks = item
        summed = jnp.zeros((SITES, CHANNELS), jnp.float32)
        for offset in range(OFFSETS):
            summed = summed + jnp.dot(ext_slab[picks[:, offset]], weight[offset], preferred_element_type=jnp.float32)
        return summed
    return lax.map(one_slab, (extended, neighbours))

def backprop_all(extended, neighbours, weight, grad_out):

    def one_slab(kernel_acc, item):
        ext_slab, picks, grad_slab = item
        ext_grad = jnp.zeros((SITES + 2 * RIM + 1, CHANNELS), jnp.float32)
        for offset in range(OFFSETS):
            picked = ext_slab[picks[:, offset]]
            kernel_acc = kernel_acc.at[offset].add(jnp.dot(picked.T, grad_slab, preferred_element_type=jnp.float32))
            back = jnp.dot(grad_slab, weight[offset].T, preferred_element_type=jnp.float32)
            ext_grad = ext_grad.at[picks[:, offset]].add(back)
        return (kernel_acc, ext_grad)
    start = jnp.zeros((OFFSETS, CHANNELS, CHANNELS), jnp.float32)
    return lax.scan(one_slab, start, (extended, neighbours, grad_out))

def retract_all(ext_grad, low_faces, high_faces):
    groups = ext_grad.shape[0]
    own_rows = ext_grad[:, :SITES]
    to_below = ext_grad[:, SITES:SITES + RIM].reshape(N_DP, N_SLAB, RIM, CHANNELS)
    to_above = ext_grad[:, SITES + RIM:SITES + 2 * RIM].reshape(N_DP, N_SLAB, RIM, CHANNELS)
    zero_slab = jnp.zeros((N_DP, 1, RIM, CHANNELS), jnp.float32)
    got_above = jnp.concatenate([to_below[:, 1:], zero_slab], 1).reshape(groups, RIM, CHANNELS)
    got_below = jnp.concatenate([zero_slab, to_above[:, :-1]], 1).reshape(groups, RIM, CHANNELS)
    own_rows = jax.vmap(lambda o, p, v: o.at[p].add(v))(own_rows, high_faces, got_above)
    own_rows = jax.vmap(lambda o, p, v: o.at[p].add(v))(own_rows, low_faces, got_below)
    return own_rows

def reference(features, counts, neighbours, low_faces, high_faces, weight_one, weight_two, cotangent):
    groups = N_DP * N_SLAB
    live_mask = (jnp.arange(SITES, dtype=jnp.int32)[None, :] < counts[:, None]).astype(jnp.float32)[:, :, None]
    grouped = features.reshape(groups, SITES, CHANNELS)
    picks = neighbours.reshape(groups, SITES, OFFSETS)
    lows = low_faces.reshape(groups, RIM)
    highs = high_faces.reshape(groups, RIM)
    masked = (grouped * live_mask).astype(jnp.bfloat16)
    ext_one = extend_all(masked, lows, highs)
    first_pre = convolve_all(ext_one, picks, weight_one)
    hidden = (jax.nn.gelu(first_pre) * live_mask).astype(jnp.bfloat16)
    ext_two = extend_all(hidden, lows, highs)
    second_pre = convolve_all(ext_two, picks, weight_two)
    response = (second_pre * live_mask).astype(jnp.bfloat16)
    out_grad = (cotangent.reshape(groups, SITES, CHANNELS) * live_mask).astype(jnp.bfloat16)
    second_sum, hidden_ext_grad = backprop_all(ext_two, picks, weight_two, out_grad)
    hidden_grad = retract_all(hidden_ext_grad, lows, highs)
    pullback = jax.vjp(jax.nn.gelu, first_pre)[1]
    pre_grad = pullback(hidden_grad * live_mask)[0].astype(jnp.bfloat16)
    first_sum, input_ext_grad = backprop_all(ext_one, picks, weight_one, pre_grad)
    input_grad = (retract_all(input_ext_grad, lows, highs) * live_mask).astype(jnp.bfloat16)
    scaling = 1.0 / math.sqrt(ROWS)
    first_grad = (first_sum * scaling).astype(jnp.bfloat16)
    second_grad = (second_sum * scaling).astype(jnp.bfloat16)
    return (response.reshape(ROWS, CHANNELS), input_grad.reshape(ROWS, CHANNELS), first_grad, second_grad)
```

```python
import math

import jax
import jax.numpy as jnp
from jax import lax
from jax.experimental import pallas as pl
from jax.experimental.pallas import tpu as pltpu
from jax.sharding import Mesh, PartitionSpec as P

AXES = ("dp", "y", "x", "zh", "core")
SLAB = ("y", "x", "zh", "core")
PLANE = ("y", "x")
DEPTH = ("dp", "zh")
BF = jnp.bfloat16
F32 = jnp.float32
WIDE = 256
TILE = 16


def dot(a, b, contract=(1, 0), exact=False):
    return lax.dot_general(
        a,
        b,
        (((contract[0],), (contract[1],)), ((), ())),
        preferred_element_type=F32,
        precision=lax.Precision.HIGHEST if exact else None,
    )


def live_rows(counts_ref, sites):
    return lax.broadcasted_iota(jnp.int32, (sites, 1), 0) < counts_ref[0]


def face_sites(faces_ref, sites):
    row = faces_ref[...]
    return (lax.broadcasted_iota(jnp.int32, (sites, row.shape[1]), 0) == row).astype(F32)


def pick_matrix(nb_ref, offset):
    sites = nb_ref.shape[0]
    column = nb_ref[:, offset : offset + 1]
    lanes = lax.broadcasted_iota(jnp.int32, (sites, WIDE), 1)
    return jnp.where(lanes == column, 1.0, 0.0).astype(BF)


def spread(grad, picks, w_ref, kept):
    turned = grad.T.astype(BF)
    offsets = w_ref.shape[0]
    total = jnp.zeros((w_ref.shape[1], WIDE), F32)
    for k in range(offsets):
        kept[k] = dot(turned, picks(k)).astype(BF)
        total = total + dot(w_ref[k], kept[k])
    return total.T


def gather_conv(extended, picks, w_ref):
    total = jnp.zeros((w_ref.shape[1], w_ref.shape[2]), F32)
    for k in range(w_ref.shape[0]):
        total = total + dot(dot(picks(k), extended).astype(BF), w_ref[k])
    return total


def kernel_grad(extended, kept, out_ref):
    turned = extended.astype(F32).T.astype(BF)
    offsets = kept.shape[0]
    for k in range(offsets):
        out_ref[k] = dot(turned, kept[k], (1, 1)).astype(BF)
    out_ref[offsets] = jnp.zeros(out_ref.shape[1:], BF)


def extend(values, below, above):
    rim = below.shape[0]
    pad = jnp.zeros((WIDE - values.shape[0] - 2 * rim, values.shape[1]), F32)
    return jnp.concatenate([values, below, above, pad], 0).astype(BF)


def send_rows(values, ext_grad, low, high, up_ref, down_ref, sites):
    rim = low.shape[1]
    up_ref[:rim] = dot(high.T.astype(BF), values)
    up_ref[rim:] = ext_grad[sites + rim : sites + 2 * rim]
    down_ref[:rim] = dot(low.T.astype(BF), values)
    down_ref[rim:] = ext_grad[sites : sites + rim]


def retract(own, below_ref, above_ref, low, high):
    rim = low.shape[1]
    own = own + dot(high, above_ref[rim:], exact=True)
    return own + dot(low, below_ref[rim:], exact=True)


def first_kernel(
    counts, feat, nb, low_ref, high_ref, cot, w_two, up, down, own, kept
):
    sites = feat.shape[0]
    live = live_rows(counts, sites)
    low, high = face_sites(low_ref, sites), face_sites(high_ref, sites)
    masked = jnp.where(live, feat[...].astype(F32), 0.0).astype(BF)
    out_grad = jnp.where(live, cot[...].astype(F32), 0.0)
    ext_grad = spread(out_grad, lambda k: pick_matrix(nb, k), w_two, kept)
    own[...] = ext_grad[:sites]
    send_rows(masked, ext_grad, low, high, up, down, sites)


def second_kernel(
    counts, feat, nb, low_ref, high_ref, below, above, hidden_own, w_one,
    up, down, own, hidden_ref, sums, picks, kept,
):
    sites = feat.shape[0]
    rim = low_ref.shape[1]
    live = live_rows(counts, sites)
    low, high = face_sites(low_ref, sites), face_sites(high_ref, sites)
    for k in range(w_one.shape[0]):
        picks[k] = pick_matrix(nb, k)
    masked = jnp.where(live, feat[...].astype(F32), 0.0)
    extended = extend(masked, below[:rim], above[:rim])
    x = gather_conv(extended, lambda k: picks[k], w_one)
    slope = math.sqrt(2.0 / math.pi)
    t = jnp.tanh(slope * (x + 0.044715 * (x * x * x)))
    cdf = 0.5 * (1.0 + t)
    hidden = jnp.where(live, x * cdf, 0.0).astype(BF)
    hidden_ref[...] = hidden
    bend = cdf + 0.5 * x * (1.0 - t * t) * (slope * (1.0 + 3 * 0.044715 * (x * x)))
    hidden_grad = retract(hidden_own[...], below, above, low, high)
    pre_grad = jnp.where(live, bend * hidden_grad, 0.0)
    ext_grad = spread(pre_grad, lambda k: picks[k], w_one, kept)
    own[...] = ext_grad[:sites]
    send_rows(hidden, ext_grad, low, high, up, down, sites)
    kernel_grad(extended, kept, sums)


def third_kernel(
    counts, hidden, nb, low_ref, high_ref, below, above, input_own, w_two, kept,
    response, input_grad, sums,
):
    sites = hidden.shape[0]
    rim = low_ref.shape[1]
    live = live_rows(counts, sites)
    low, high = face_sites(low_ref, sites), face_sites(high_ref, sites)
    extended = extend(hidden[...].astype(F32), below[:rim], above[:rim])
    kernel_grad(extended, kept, sums)
    second_pre = gather_conv(extended, lambda k: pick_matrix(nb, k), w_two)
    response[...] = jnp.where(live, second_pre, 0.0).astype(BF)
    grad = retract(input_own[...], below, above, low, high)
    input_grad[...] = jnp.where(live, grad, 0.0).astype(BF)


def call(kernel, outs, scratch=(), **cost):
    def run(*args):
        specs = [pl.BlockSpec(memory_space=pltpu.SMEM)]
        specs += [pl.BlockSpec(memory_space=pltpu.VMEM)] * (len(args) - 1)
        return pl.pallas_call(
            kernel,
            out_shape=[jax.ShapeDtypeStruct(s, d) for s, d in outs],
            in_specs=specs,
            out_specs=[pl.BlockSpec(memory_space=pltpu.VMEM)] * len(outs),
            scratch_shapes=[pltpu.VMEM(s, d) for s, d in scratch],
            compiler_params=pltpu.CompilerParams(vmem_limit_bytes=40 * 2**20),
        )(*args)

    return run


def neighbours_of(up, down):
    last = lax.axis_size(SLAB) - 1
    below = lax.ppermute(up, SLAB, [(i, i + 1) for i in range(last)])
    above = lax.ppermute(down, SLAB, [(i + 1, i) for i in range(last)])
    return below, above


def swap(block, axis):
    return lax.all_to_all(block, axis, 0, 0, tiled=True)


def total_of(parts):
    return jnp.sum(parts.astype(F32), 0)


def scatter_plane(sums):
    rows, channels = sums.shape[0] * sums.shape[1], sums.shape[2]
    cores, plane = lax.axis_size("core"), lax.axis_size(PLANE)
    halves = swap(sums.reshape(cores, rows // cores, channels), "core")
    share = total_of(halves).astype(BF).reshape(plane, -1, channels)
    return total_of(swap(share, PLANE))


def finish(shares, scaling, offsets, channels):
    grads, rows = len(shares), shares[0].shape[0]
    depth, plane, cores = lax.axis_size(DEPTH), lax.axis_size(PLANE), lax.axis_size("core")
    parts = jnp.stack(shares).reshape(grads, depth, rows // depth, channels)
    parts = parts.transpose(1, 0, 2, 3)
    mine = (total_of(swap(parts, DEPTH)) * scaling).astype(BF)
    column = swap(jnp.broadcast_to(mine, (depth, *mine.shape)), DEPTH)
    column = column.transpose(1, 0, 2, 3).reshape(grads, rows, channels)
    whole = swap(jnp.broadcast_to(column, (plane, *column.shape)), PLANE)
    whole = swap(jnp.broadcast_to(whole, (cores, *whole.shape)), "core")
    whole = whole.transpose(2, 0, 1, 3, 4).reshape(grads, -1, channels, channels)
    return [whole[g, :offsets] for g in range(grads)]


def on_device(feat, counts, nb, low, high, w_one, w_two, cot):
    sites, channels = feat.shape
    offsets, rim = nb.shape[1], low.shape[0]
    scaling = 1.0 / math.sqrt(lax.axis_size(AXES) * sites)
    low, high = low.reshape(1, rim), high.reshape(1, rim)
    rims = ((2 * rim, channels), F32)
    field = ((sites, channels), F32)
    kept = ((offsets, channels, WIDE), BF)
    picks = ((offsets, sites, WIDE), BF)
    sums = ((offsets + 1, channels, channels), BF)
    flat = ((sites, channels), BF)
    up, down, hidden_own, kept_two = call(first_kernel, (rims, rims, field, kept))(
        counts, feat, nb, low, high, cot, w_two
    )
    below, above = neighbours_of(up, down)
    up, down, input_own, hidden, sums_one = call(
        second_kernel, (rims, rims, field, flat, sums), (picks, kept)
    )(counts, feat, nb, low, high, below, above, hidden_own, w_one)
    below, above = neighbours_of(up, down)
    share_one = scatter_plane(sums_one)
    response, input_grad, sums_two = call(third_kernel, (flat, flat, sums))(
        counts, hidden, nb, low, high, below, above, input_own, w_two, kept_two
    )
    share_two = scatter_plane(sums_two)
    first, second = finish((share_one, share_two), scaling, offsets, channels)
    return response, input_grad, first, second


def solution(mesh):
    groups, slabs = mesh.devices.shape
    side = {64: 4, 16: 2, 4: 1}[slabs]
    fine = Mesh(mesh.devices.reshape(groups, side, side, 2, 2), AXES)
    rows, row = P(AXES, None), P(AXES)
    return jax.shard_map(
        on_device,
        mesh=fine,
        in_specs=(rows, row, rows, row, row, P(), P(), rows),
        out_specs=(rows, rows, P(), P()),
        check_vma=False,
    )
```

```python
import math

import jax
import jax.numpy as jnp
from jax import lax
from jax.experimental import pallas as pl
from jax.experimental.pallas import tpu as pltpu
from jax.sharding import Mesh, PartitionSpec as P

AXES = ("dp", "y", "x", "zh", "core")
SLAB = ("y", "x", "zh", "core")
PLANE = ("y", "x")
DEPTH = ("dp", "zh")
BF = jnp.bfloat16
F32 = jnp.float32
WIDE = 256
NOWHERE = 255.0


def dot(a, b, contract=(1, 0), exact=False):
    return lax.dot_general(
        a,
        b,
        (((contract[0],), (contract[1],)), ((), ())),
        preferred_element_type=F32,
        precision=lax.Precision.HIGHEST if exact else None,
    )


def iota(shape, dim):
    return lax.broadcasted_iota(jnp.int32, shape, dim).astype(F32)


def live_rows(counts_ref, sites):
    return lax.broadcasted_iota(jnp.int32, (sites, 1), 0) < counts_ref[0]


def face_sites(row, sites):
    return (iota((sites, row.shape[1]), 0) == row).astype(F32)


def pick_matrix(columns, k):
    sites = columns.shape[0]
    return jnp.where(iota((sites, WIDE), 1) == columns[:, k : k + 1], 1.0, 0.0).astype(BF)


def gather_conv(extended, picks, w_ref):
    total = jnp.zeros((w_ref.shape[1], w_ref.shape[2]), F32)
    for k in range(w_ref.shape[0]):
        total = total + dot(dot(picks(k), extended).astype(BF), w_ref[k])
    return total


def extend(values, below, above):
    rim = below.shape[0]
    pad = jnp.zeros((WIDE - values.shape[0] - 2 * rim, values.shape[1]), F32)
    return jnp.concatenate([values, below, above, pad], 0).astype(BF)


def fetch(sources, targets, sems):
    copies = [
        pltpu.make_async_copy(s, t, sems.at[i])
        for i, (s, t) in enumerate(zip(sources, targets))
    ]
    for copy in copies:
        copy.start()
    return copies


def pack_kernel(
    counts, feat_h, cot_h, map_h, low_h, high_h, up, down, masked_ref, faces,
    feat, cot, table, low_s, high_s, sems,
):
    for copy in fetch(
        (feat_h, cot_h, map_h, low_h, high_h), (feat, cot, table, low_s, high_s), sems
    ):
        copy.wait()
    sites, rim = feat.shape[0], low_s.shape[1]
    live = live_rows(counts, sites)
    masked = jnp.where(live, feat[...].astype(F32), 0.0).astype(BF)
    masked_ref[...] = masked
    grad = jnp.where(live, cot[...].astype(F32), 0.0).astype(BF)
    offsets = table.shape[0]
    names = jnp.concatenate(
        [table[...].astype(F32), jnp.full((rim - offsets, sites), NOWHERE, F32)], 0
    ).astype(BF)
    faces[0:1] = low_s[...].astype(F32)
    faces[1:2] = high_s[...].astype(F32)
    for out, row in ((up, faces[1:2]), (down, faces[0:1])):
        out[:sites] = grad
        picks = face_sites(row, sites).T.astype(BF)
        out[sites : sites + rim] = dot(picks, masked).astype(BF)
        out[sites + rim :] = names


def sites_of(names, first, row):
    found = jnp.full(names.shape, NOWHERE, F32)
    for j in range(row.shape[1]):
        found = jnp.where(names == first + j, row[:, j : j + 1], found)
    return found


def main_kernel(
    counts, masked, own, faces, below, above, w_one_h, w_two_h,
    up, down, own_grad, hidden_ref, mine, theirs,
    w_one, w_two, picks, held, kept, sems,
):
    copies = fetch((w_one_h, w_two_h), (w_one, w_two), sems)
    offsets, channels = w_one.shape[0], w_one.shape[1]
    sites, rim = masked.shape[0], faces.shape[1]
    live = live_rows(counts, sites)
    low_row, high_row = faces[0:1], faces[1:2]
    names = own[sites + rim :].astype(F32)
    columns = names.T
    for k in range(offsets):
        picks[k] = pick_matrix(columns, k)
    rims = slice(sites, sites + rim)
    extended = extend(
        masked[...].astype(F32), below[rims].astype(F32), above[rims].astype(F32)
    )

    above_names = sites_of(above[sites + rim :].astype(F32), sites, high_row)
    below_names = sites_of(below[sites + rim :].astype(F32), sites + rim, low_row)
    names = jnp.concatenate([names, above_names, below_names], 1)
    grads = jnp.concatenate([own[:sites], above[:sites], below[:sites]], 0)
    rows = iota((sites, 3 * sites), 0)
    for k in range(offsets):
        hits = jnp.where(rows == names[k : k + 1], 1.0, 0.0).astype(BF)
        held[k] = dot(hits, grads).astype(BF)
    copies[0].wait()
    x = gather_conv(extended, lambda k: picks[k], w_one)
    copies[1].wait()
    hidden_grad = jnp.zeros((sites, channels), F32)
    for k in range(offsets):
        hidden_grad = hidden_grad + dot(held[k], w_two[k], (1, 1))

    slope = math.sqrt(2.0 / math.pi)
    t = jnp.tanh(slope * (x + 0.044715 * (x * x * x)))
    cdf = 0.5 * (1.0 + t)
    hidden = jnp.where(live, x * cdf, 0.0)
    hidden_ref[...] = hidden.astype(BF)
    bend = cdf + 0.5 * x * (1.0 - t * t) * (slope * (1.0 + 3 * 0.044715 * (x * x)))
    pre_grad = jnp.where(live, bend * hidden_grad, 0.0)

    turned = pre_grad.T.astype(BF)
    extended_t = extended.astype(F32).T.astype(BF)
    hidden_t = hidden.T.astype(BF)
    total = jnp.zeros((channels, WIDE), F32)
    first_is_mine = lax.axis_index("core") == 0
    for k in range(offsets):
        kept[k] = dot(turned, picks[k]).astype(BF)
        total = total + dot(w_one[k], kept[k])
        first = dot(extended_t, kept[k], (1, 1))
        second = dot(hidden_t, held[k])
        mine[k] = jnp.where(first_is_mine, first, second).astype(BF)
        theirs[k] = jnp.where(first_is_mine, second, first).astype(BF)
    mine[offsets] = jnp.zeros((channels, channels), BF)
    theirs[offsets] = jnp.zeros((channels, channels), BF)
    ext_grad = total.T
    own_grad[...] = ext_grad[:sites]
    low, high = face_sites(low_row, sites), face_sites(high_row, sites)
    up[:rim] = dot(high.T.astype(BF), hidden.astype(BF))
    up[rim:] = ext_grad[sites + rim : sites + 2 * rim]
    down[:rim] = dot(low.T.astype(BF), hidden.astype(BF))
    down[rim:] = ext_grad[sites : sites + rim]


def last_kernel(
    counts, hidden, own, faces, below, above, own_grad, w_two_h,
    response, input_grad, w_two, sems,
):
    copies = fetch((w_two_h,), (w_two,), sems)
    sites, rim = hidden.shape[0], faces.shape[1]
    live = live_rows(counts, sites)
    low, high = face_sites(faces[0:1], sites), face_sites(faces[1:2], sites)
    grad = own_grad[...] + dot(high, above[rim:], exact=True)
    grad = grad + dot(low, below[rim:], exact=True)
    input_grad[...] = jnp.where(live, grad, 0.0).astype(BF)
    columns = own[sites + rim :].astype(F32).T
    extended = extend(hidden[...].astype(F32), below[:rim], above[:rim])
    copies[0].wait()
    second_pre = gather_conv(extended, lambda k: pick_matrix(columns, k), w_two)
    response[...] = jnp.where(live, second_pre, 0.0).astype(BF)


def call(kernel, places, outs, scratch, copies, us):
    memory = {"s": pltpu.SMEM, "v": pltpu.VMEM, "h": pltpu.HBM}
    return pl.pallas_call(
        kernel,
        out_shape=[jax.ShapeDtypeStruct(s, d) for s, d in outs],
        in_specs=[pl.BlockSpec(memory_space=memory[p]) for p in places],
        out_specs=[pl.BlockSpec(memory_space=pltpu.VMEM)] * len(outs),
        scratch_shapes=[pltpu.VMEM(s, d) for s, d in scratch]
        + [pltpu.SemaphoreType.DMA((copies,))],
        compiler_params=pltpu.CompilerParams(vmem_limit_bytes=40 * 2**20),
        cost_estimate=pl.CostEstimate(
            flops=0, bytes_accessed=int(us * 3e6), transcendentals=0
        ),
    )


def exchange(up, down):
    last = lax.axis_size(SLAB) - 1
    below = lax.ppermute(up, SLAB, [(i, i + 1) for i in range(last)])
    above = lax.ppermute(down, SLAB, [(i + 1, i) for i in range(last)])
    return below, above


def swap(block, axis):
    return lax.all_to_all(block, axis, 0, 0, tiled=True)


def other_core(block):
    return lax.ppermute(block, "core", [(0, 1), (1, 0)])


def on_device(feat, counts, nb, low, high, w_one, w_two, cot):
    sites, channels = feat.shape
    offsets, rim = nb.shape[1], low.shape[0]
    scaling = 1.0 / math.sqrt(lax.axis_size(AXES) * sites)
    flat = ((sites, channels), BF)
    field = ((sites, channels), F32)
    letter = ((sites + 2 * rim, channels), BF)
    ends = ((2 * rim, channels), F32)
    weight = ((offsets, channels, channels), BF)
    sums = ((offsets + 1, channels, channels), BF)
    row = ((1, rim), jnp.int32)
    up, down, masked, faces = call(
        pack_kernel, "shhhhh", (letter, letter, flat, ((2, rim), F32)),
        (flat, flat, ((offsets, sites), jnp.int32), row, row), 5, 1,
    )(counts, feat, cot, nb.T, low.reshape(1, rim), high.reshape(1, rim))
    below, above = exchange(up, down)
    picks = ((offsets, sites, WIDE), BF)
    kept = ((offsets, channels, WIDE), BF)
    up_two, down_two, own_grad, hidden, mine, theirs = call(
        main_kernel, "svvvvvhh", (ends, ends, field, flat, sums, sums),
        (weight, weight, picks, weight, kept), 2, 5,
    )(counts, masked, up, faces, below, above, w_one, w_two)

    depth, plane = lax.axis_size(DEPTH), lax.axis_size(PLANE)
    share = (mine.astype(F32) + other_core(theirs).astype(F32)).astype(BF)
    share, up_two, down_two = lax.optimization_barrier((share, up_two, down_two))
    parts = swap(share.reshape(plane, -1, channels), PLANE)
    below, above = exchange(up_two, down_two)
    parts = jnp.sum(parts.astype(F32), 0).reshape(depth, -1, channels)
    total = jnp.sum(swap(parts, DEPTH), 0) * scaling
    response, input_grad = call(
        last_kernel, "svvvvvvh", (flat, flat), (weight,), 1, 3
    )(counts, hidden, up, faces, below, above, own_grad, w_two)

    total = total.astype(BF)
    column = swap(jnp.broadcast_to(total, (depth, *total.shape)), DEPTH)
    column = column.reshape(-1, channels)
    whole = swap(jnp.broadcast_to(column, (plane, *column.shape)), PLANE)
    whole = whole.reshape(offsets + 1, channels, channels)
    other = other_core(whole)
    first_is_mine = lax.axis_index("core") == 0
    first = jnp.where(first_is_mine, whole, other)[:offsets]
    second = jnp.where(first_is_mine, other, whole)[:offsets]
    return response, input_grad, first, second


def solution(mesh):
    groups, slabs = mesh.devices.shape
    side = {64: 4, 16: 2, 4: 1}[slabs]
    fine = Mesh(mesh.devices.reshape(groups, side, side, 2, 2), AXES)
    rows, row = P(AXES, None), P(AXES)
    return jax.shard_map(
        on_device,
        mesh=fine,
        in_specs=(rows, row, rows, row, row, P(), P(), rows),
        out_specs=(rows, rows, P(), P()),
        check_vma=False,
    )
```

```python
import math

import jax
import jax.numpy as jnp
from jax import lax
from jax.experimental import pallas as pl
from jax.experimental.pallas import tpu as pltpu
from jax.sharding import Mesh, PartitionSpec as P

AXES = ("dp", "y", "x", "zh", "core")
SLAB = ("y", "x", "zh", "core")
PLANE = ("y", "x")
DEPTH = ("dp", "zh")
BF = jnp.bfloat16
F32 = jnp.float32
WIDE = 256
NOWHERE = 255.0


def dot(a, b, contract=(1, 0), exact=False):
    return lax.dot_general(
        a,
        b,
        (((contract[0],), (contract[1],)), ((), ())),
        preferred_element_type=F32,
        precision=lax.Precision.HIGHEST if exact else None,
    )


def iota(shape, dim):
    return lax.broadcasted_iota(jnp.int32, shape, dim).astype(F32)


def live_rows(counts_ref, sites):
    return lax.broadcasted_iota(jnp.int32, (sites, 1), 0) < counts_ref[0]


def face_sites(row, sites):
    return (iota((sites, row.shape[1]), 0) == row).astype(F32)


def pick_matrix(columns, k):
    sites = columns.shape[0]
    return jnp.where(iota((sites, WIDE), 1) == columns[:, k : k + 1], 1.0, 0.0).astype(BF)


def gather_conv(extended, picks, w_ref):
    total = jnp.zeros((w_ref.shape[1], w_ref.shape[2]), F32)
    for k in range(w_ref.shape[0]):
        total = total + dot(dot(picks(k), extended).astype(BF), w_ref[k])
    return total


def extend(values, below, above):
    rim = below.shape[0]
    pad = jnp.zeros((WIDE - values.shape[0] - 2 * rim, values.shape[1]), F32)
    return jnp.concatenate([values, below, above, pad], 0).astype(BF)


def fetch(sources, targets, sems):
    copies = [
        pltpu.make_async_copy(s, t, sems.at[i])
        for i, (s, t) in enumerate(zip(sources, targets))
    ]
    for copy in copies:
        copy.start()
    return copies


def near_is_above():
    return lax.axis_index("core") == 0


def near_and_far(faces):
    above = near_is_above()
    low, high = faces[0:1], faces[1:2]
    return jnp.where(above, high, low), jnp.where(above, low, high)


def pack_kernel(
    counts, feat_h, cot_h, map_h, low_h, high_h, near, far, faces,
    feat, cot, table, low_s, high_s, sems,
):
    for copy in fetch(
        (feat_h, cot_h, map_h, low_h, high_h), (feat, cot, table, low_s, high_s), sems
    ):
        copy.wait()
    sites, rim = feat.shape[0], low_s.shape[1]
    live = live_rows(counts, sites)
    masked = jnp.where(live, feat[...].astype(F32), 0.0).astype(BF)
    grad = jnp.where(live, cot[...].astype(F32), 0.0).astype(BF)
    offsets = table.shape[0]
    names = jnp.concatenate(
        [table[...].astype(F32), jnp.full((rim - offsets, sites), NOWHERE, F32)], 0
    ).astype(BF)
    faces[0:1] = low_s[...].astype(F32)
    faces[1:2] = high_s[...].astype(F32)
    for out, row in zip((near, far), near_and_far(faces)):
        out[:sites] = grad
        picks = face_sites(row, sites).T.astype(BF)
        out[sites : sites + rim] = dot(picks, masked).astype(BF)
        out[sites + rim :] = names


def stage_kernel(
    counts, feat, own, faces_in, w_one_in, w_two_in,
    masked, grad, names, faces, picks, w_one, w_two, sems,
):
    sites, rim = feat.shape[0], faces.shape[1]
    live = live_rows(counts, sites)
    masked[...] = jnp.where(live, feat[...].astype(F32), 0.0).astype(BF)
    grad[...] = own[:sites]
    names[...] = own[sites + rim :].astype(F32)
    faces[...] = faces_in[...]
    columns = names[...].T
    for k in range(picks.shape[0]):
        picks[k] = pick_matrix(columns, k)
        w_one[k] = w_one_in[k]
        w_two[k] = w_two_in[k]


def sites_of(names, first, row):
    found = jnp.full(names.shape, NOWHERE, F32)
    for j in range(row.shape[1]):
        found = jnp.where(names == first + j, row[:, j : j + 1], found)
    return found


def lanes(k, width, n=1):
    return slice(k * width, (k + n) * width)


def back(held, w_ref, rows):
    offsets, channels = w_ref.shape[0], w_ref.shape[1]
    total = jnp.zeros((rows, channels), F32)
    for k in range(0, offsets, 2):
        n = min(2, offsets - k)
        weight = jnp.concatenate([w_ref[k + j] for j in range(n)], 1)
        total = total + dot(held[:, lanes(k, w_ref.shape[2], n)], weight, (1, 1))
    return total


def main_kernel(
    counts, masked, own_grads, own_names, faces, picks, w_one, w_two, near, far,
    near_out, far_out, own_grad, hidden_ref, mine, theirs,
    picked, held, kept, sems,
):
    offsets, channels = w_one.shape[0], w_one.shape[1]
    sites, rim = masked.shape[0], faces.shape[1]
    live = live_rows(counts, sites)
    above = near_is_above()
    near_row, far_row = near_and_far(faces)
    rims = slice(sites, sites + rim)
    near_rim, far_rim = near[rims].astype(F32), far[rims].astype(F32)
    extended = extend(
        masked[...].astype(F32),
        jnp.where(above, far_rim, near_rim),
        jnp.where(above, near_rim, far_rim),
    )
    for k in range(offsets):
        picked[:, lanes(k, channels)] = dot(picks[k], extended).astype(BF)
    x = dot(picked[...], w_one[...].reshape(offsets * channels, channels))

    up_first, down_first = float(sites), float(sites + rim)
    near_first = jnp.where(above, up_first, down_first)
    far_first = jnp.where(above, down_first, up_first)
    names = jnp.concatenate(
        [
            own_names[...],
            sites_of(near[sites + rim :].astype(F32), near_first, near_row),
            sites_of(far[sites + rim :].astype(F32), far_first, far_row),
        ],
        1,
    )
    grads = jnp.concatenate([own_grads[...], near[:sites], far[:sites]], 0)
    rows = iota((sites, 3 * sites), 0)
    for k in range(offsets):
        hits = jnp.where(rows == names[k : k + 1], 1.0, 0.0).astype(BF)
        held[:, lanes(k, channels)] = dot(hits, grads).astype(BF)
    hidden_grad = back(held, w_two, sites)

    slope = math.sqrt(2.0 / math.pi)
    t = jnp.tanh(slope * (x + 0.044715 * (x * x * x)))
    cdf = 0.5 * (1.0 + t)
    hidden = jnp.where(live, x * cdf, 0.0)
    hidden_ref[...] = hidden.astype(BF)
    bend = cdf + 0.5 * x * (1.0 - t * t) * (slope * (1.0 + 3 * 0.044715 * (x * x)))
    pre_grad = jnp.where(live, bend * hidden_grad, 0.0).astype(BF)

    extended_t = extended.astype(F32).T.astype(BF)
    hidden_t = hidden.T.astype(BF)
    rows = iota((WIDE, sites), 0)
    for k in range(offsets):
        hits = jnp.where(rows == names[k : k + 1, :sites], 1.0, 0.0).astype(BF)
        kept[:, lanes(k, channels)] = dot(hits, pre_grad).astype(BF)
    ext_grad = back(kept, w_one, WIDE)
    own_grad[...] = ext_grad[:sites]
    to_above, to_below = ext_grad[sites + rim : sites + 2 * rim], ext_grad[rims]
    near_pick = face_sites(near_row, sites).T.astype(BF)
    far_pick = face_sites(far_row, sites).T.astype(BF)
    near_out[:rim] = dot(near_pick, hidden.astype(BF))
    near_out[rim:] = jnp.where(above, to_above, to_below)
    far_out[:rim] = dot(far_pick, hidden.astype(BF))
    far_out[rim:] = jnp.where(above, to_below, to_above)
    first_is_mine = lax.axis_index("core") == 0
    for k in range(0, offsets, 2):
        n = min(2, offsets - k)
        first = dot(extended_t, kept[:, lanes(k, channels, n)])
        second = dot(hidden_t, held[:, lanes(k, channels, n)])
        for j in range(n):
            a, b = first[:, lanes(j, channels)], second[:, lanes(j, channels)]
            mine[k + j] = jnp.where(first_is_mine, a, b).astype(BF)
            theirs[k + j] = jnp.where(first_is_mine, b, a).astype(BF)
    mine[offsets] = jnp.zeros((channels, channels), BF)
    theirs[offsets] = jnp.zeros((channels, channels), BF)


def last_kernel(
    counts, hidden, faces, near, far, own_grad, picks, w_two,
    response, input_grad, picked, sems,
):
    sites, rim = hidden.shape[0], faces.shape[1]
    offsets, channels = w_two.shape[0], w_two.shape[1]
    live = live_rows(counts, sites)
    above = near_is_above()
    near_row, far_row = near_and_far(faces)
    grad = own_grad[...] + dot(face_sites(near_row, sites), near[rim:], exact=True)
    grad = grad + dot(face_sites(far_row, sites), far[rim:], exact=True)
    input_grad[...] = jnp.where(live, grad, 0.0).astype(BF)
    extended = extend(
        hidden[...].astype(F32),
        jnp.where(above, far[:rim], near[:rim]),
        jnp.where(above, near[:rim], far[:rim]),
    )
    for k in range(offsets):
        picked[:, lanes(k, channels)] = dot(picks[k], extended).astype(BF)
    second_pre = dot(picked[...], w_two[...].reshape(offsets * channels, channels))
    response[...] = jnp.where(live, second_pre, 0.0).astype(BF)


def call(kernel, places, outs, scratch, copies, us, limit=32):
    memory = {"s": pltpu.SMEM, "v": pltpu.VMEM, "h": pltpu.HBM}
    return pl.pallas_call(
        kernel,
        out_shape=[jax.ShapeDtypeStruct(s, d) for s, d in outs],
        in_specs=[pl.BlockSpec(memory_space=memory[p]) for p in places],
        out_specs=[pl.BlockSpec(memory_space=pltpu.VMEM)] * len(outs),
        scratch_shapes=[pltpu.VMEM(s, d) for s, d in scratch]
        + [pltpu.SemaphoreType.DMA((copies,))],
        compiler_params=pltpu.CompilerParams(vmem_limit_bytes=limit * 2**20),
        cost_estimate=pl.CostEstimate(
            flops=0, bytes_accessed=int(us * 3e6), transcendentals=0
        ),
    )


def exchange(near, far):
    last = lax.axis_size(SLAB) - 1
    pairs = [p for i in range(1, last, 2) for p in ((i, i + 1), (i + 1, i))]
    from_far = lax.ppermute(far, SLAB, pairs)
    return other_core(near), from_far


def swap(block, axis):
    return lax.all_to_all(block, axis, 0, 0, tiled=True)


def other_core(block):
    return lax.ppermute(block, "core", [(0, 1), (1, 0)])


def on_device(feat, counts, nb, low, high, w_one, w_two, cot):
    sites, channels = feat.shape
    offsets, rim = nb.shape[1], low.shape[0]
    scaling = 1.0 / math.sqrt(lax.axis_size(AXES) * sites)
    flat = ((sites, channels), BF)
    field = ((sites, channels), F32)
    letter = ((sites + 2 * rim, channels), BF)
    ends = ((2 * rim, channels), F32)
    weight = ((offsets, channels, channels), BF)
    sums = ((offsets + 1, channels, channels), BF)
    row = ((1, rim), jnp.int32)
    faces = ((2, rim), F32)
    picks = ((offsets, sites, WIDE), BF)
    broad = ((sites, offsets * channels), BF)
    near, far, sides = call(
        pack_kernel, "shhhhh", (letter, letter, faces),
        (flat, flat, ((offsets, sites), jnp.int32), row, row), 5, 1, limit=60,
    )(counts, feat, cot, nb.T, low.reshape(1, rim), high.reshape(1, rim))
    masked, grad, names, faces, picks, w_one, w_two = call(
        stage_kernel, "svvvvv",
        (flat, flat, ((rim, sites), F32), faces, picks, weight, weight), (), 1, 2,
    )(counts, feat, near, sides, w_one, w_two)
    near, far = exchange(near, far)
    near_two, far_two, own_grad, hidden, mine, theirs = call(
        main_kernel, "svvvvvvvvv", (ends, ends, field, flat, sums, sums),
        (broad, broad, ((WIDE, offsets * channels), BF)), 1, 5,
    )(counts, masked, grad, names, faces, picks, w_one, w_two, near, far)

    depth, plane = lax.axis_size(DEPTH), lax.axis_size(PLANE)
    share = (mine.astype(F32) + other_core(theirs).astype(F32)).astype(BF)
    share, near_two, far_two = lax.optimization_barrier((share, near_two, far_two))
    parts = swap(share.reshape(plane, -1, channels), PLANE)
    near, far = exchange(near_two, far_two)
    parts = jnp.sum(parts.astype(F32), 0).reshape(depth, -1, channels)
    parts, near, far = lax.optimization_barrier((parts, near, far))
    total = jnp.sum(swap(parts, DEPTH), 0) * scaling
    response, input_grad = call(
        last_kernel, "svvvvvvv", (flat, flat), (broad,), 1, 3
    )(counts, hidden, faces, near, far, own_grad, picks, w_two)
    total, response, input_grad = lax.optimization_barrier((total, response, input_grad))

    total = total.astype(BF)
    column = swap(jnp.broadcast_to(total, (depth, *total.shape)), DEPTH)
    column = column.reshape(-1, channels)
    whole = swap(jnp.broadcast_to(column, (plane, *column.shape)), PLANE)
    whole = whole.reshape(offsets + 1, channels, channels)
    other = other_core(whole)
    first_is_mine = lax.axis_index("core") == 0
    first = jnp.where(first_is_mine, whole, other)[:offsets]
    second = jnp.where(first_is_mine, other, whole)[:offsets]
    return response, input_grad, first, second


def solution(mesh):
    groups, slabs = mesh.devices.shape
    side = {64: 4, 16: 2, 4: 1}[slabs]
    fine = Mesh(mesh.devices.reshape(groups, side, side, 2, 2), AXES)
    rows, row = P(AXES, None), P(AXES)
    return jax.shard_map(
        on_device,
        mesh=fine,
        in_specs=(rows, row, rows, row, row, P(), P(), rows),
        out_specs=(rows, rows, P(), P()),
        check_vma=False,
    )
```

```python
import math

import jax
import jax.numpy as jnp
from jax import lax
from jax.experimental import pallas as pl
from jax.experimental.pallas import tpu as pltpu
from jax.sharding import Mesh, PartitionSpec as P

AXES = ("dp", "y", "x", "zh", "core")
SLAB = ("y", "x", "zh", "core")
PLANE = ("y", "x")
DEPTH = ("dp", "zh")
BF = jnp.bfloat16
F32 = jnp.float32
WIDE = 256
NOWHERE = 255.0


def dot(a, b, contract=(1, 0), exact=False):
    return lax.dot_general(
        a,
        b,
        (((contract[0],), (contract[1],)), ((), ())),
        preferred_element_type=F32,
        precision=lax.Precision.HIGHEST if exact else None,
    )


def iota(shape, dim):
    return lax.broadcasted_iota(jnp.int32, shape, dim).astype(F32)


def live_rows(counts_ref, sites):
    return lax.broadcasted_iota(jnp.int32, (sites, 1), 0) < counts_ref[0]


def face_sites(row, sites):
    return (iota((sites, row.shape[1]), 0) == row).astype(F32)


def pick_matrix(columns, k):
    sites = columns.shape[0]
    return jnp.where(iota((sites, WIDE), 1) == columns[:, k : k + 1], 1.0, 0.0).astype(BF)


def gather_conv(extended, picks, w_ref):
    total = jnp.zeros((w_ref.shape[1], w_ref.shape[2]), F32)
    for k in range(w_ref.shape[0]):
        total = total + dot(dot(picks(k), extended).astype(BF), w_ref[k])
    return total


def extend(values, below, above):
    rim = below.shape[0]
    pad = jnp.zeros((WIDE - values.shape[0] - 2 * rim, values.shape[1]), F32)
    return jnp.concatenate([values, below, above, pad], 0).astype(BF)


def fetch(sources, targets, sems):
    copies = [
        pltpu.make_async_copy(s, t, sems.at[i])
        for i, (s, t) in enumerate(zip(sources, targets))
    ]
    for copy in copies:
        copy.start()
    return copies


def near_is_above():
    return lax.axis_index("core") == 0


def near_and_far(low, high):
    above = near_is_above()
    return jnp.where(above, high, low), jnp.where(above, low, high)


def pack_kernel(
    counts, feat_h, cot_h, map_h, low_h, high_h, near, far, faces,
    feat, cot, table, low, high, sems,
):
    for copy in fetch(
        (feat_h, cot_h, map_h, low_h, high_h), (feat, cot, table, low, high), sems
    ):
        copy.wait()
    live = live_rows(counts, feat.shape[0])
    faces[0:1] = low[...].astype(F32)
    faces[1:2] = high[...].astype(F32)
    offsets, sites = table.shape
    rim = low.shape[1]
    masked = jnp.where(live, feat[...].astype(F32), 0.0).astype(BF)
    grad = jnp.where(live, cot[...].astype(F32), 0.0).astype(BF)
    blank = jnp.full((rim - offsets, sites), NOWHERE, F32)
    names = jnp.concatenate([table[...].astype(F32), blank], 0).astype(BF)
    for out, row in zip((far, near), near_and_far(faces[1:2], faces[0:1])):
        out[:sites] = grad
        picks = face_sites(row, sites).T.astype(BF)
        out[sites : sites + rim] = dot(picks, masked).astype(BF)
        out[sites + rim :] = names


def stage_kernel(
    counts, feat, own, sides, w_one_in, w_two_in,
    masked, grad, names, faces, picks, w_one, w_two, sems,
):
    sites, rim = feat.shape[0], sides.shape[1]
    live = live_rows(counts, sites)
    masked[...] = jnp.where(live, feat[...].astype(F32), 0.0).astype(BF)
    grad[...] = own[:sites]
    names[...] = own[sites + rim :].astype(F32)
    faces[...] = sides[...]
    columns = names[...].T
    for k in range(picks.shape[0]):
        picks[k] = pick_matrix(columns, k)
        w_one[k] = w_one_in[k]
        w_two[k] = w_two_in[k]


def sites_of(names, first, row):
    found = jnp.full(names.shape, NOWHERE, F32)
    for j in range(row.shape[1]):
        found = jnp.where(names == first + j, row[:, j : j + 1], found)
    return found


def lanes(k, width, n=1):
    return slice(k * width, (k + n) * width)


def back(held, w_ref, rows):
    offsets, channels = w_ref.shape[0], w_ref.shape[1]
    total = jnp.zeros((rows, channels), F32)
    for k in range(0, offsets, 2):
        n = min(2, offsets - k)
        weight = jnp.concatenate([w_ref[k + j] for j in range(n)], 1)
        total = total + dot(held[:, lanes(k, w_ref.shape[2], n)], weight, (1, 1))
    return total


def main_kernel(
    counts, masked, own_grads, own_names, faces, picks, w_one, w_two, far, near,
    far_out, own_grad, hidden_ref, mine, theirs,
    picked, held, kept, sems,
):
    offsets, channels = w_one.shape[0], w_one.shape[1]
    sites, rim = masked.shape[0], faces.shape[1]
    live = live_rows(counts, sites)
    above = near_is_above()
    near_row, far_row = near_and_far(faces[0:1], faces[1:2])
    rims = slice(sites, sites + rim)
    near_rim, far_rim = near[rims].astype(F32), far[rims].astype(F32)
    extended = extend(
        masked[...].astype(F32),
        jnp.where(above, far_rim, near_rim),
        jnp.where(above, near_rim, far_rim),
    )
    for k in range(offsets):
        picked[:, lanes(k, channels)] = dot(picks[k], extended).astype(BF)
    x = dot(picked[...], w_one[...].reshape(offsets * channels, channels))

    up_first, down_first = float(sites), float(sites + rim)
    near_first = jnp.where(above, up_first, down_first)
    far_first = jnp.where(above, down_first, up_first)
    names = jnp.concatenate(
        [
            own_names[...],
            sites_of(near[sites + rim :].astype(F32), near_first, near_row),
            sites_of(far[sites + rim :].astype(F32), far_first, far_row),
        ],
        1,
    )
    grads = jnp.concatenate([own_grads[...], near[:sites], far[:sites]], 0)
    rows = iota((sites, 3 * sites), 0)
    for k in range(offsets):
        hits = jnp.where(rows == names[k : k + 1], 1.0, 0.0).astype(BF)
        held[:, lanes(k, channels)] = dot(hits, grads).astype(BF)
    hidden_grad = back(held, w_two, sites)

    slope = math.sqrt(2.0 / math.pi)
    t = jnp.tanh(slope * (x + 0.044715 * (x * x * x)))
    cdf = 0.5 * (1.0 + t)
    hidden = jnp.where(live, x * cdf, 0.0)
    hidden_ref[...] = hidden.astype(BF)
    bend = cdf + 0.5 * x * (1.0 - t * t) * (slope * (1.0 + 3 * 0.044715 * (x * x)))
    pre_grad = jnp.where(live, bend * hidden_grad, 0.0).astype(BF)

    extended_t = extended.astype(F32).T.astype(BF)
    hidden_t = hidden.T.astype(BF)
    rows = iota((WIDE, sites), 0)
    for k in range(offsets):
        hits = jnp.where(rows == names[k : k + 1, :sites], 1.0, 0.0).astype(BF)
        kept[:, lanes(k, channels)] = dot(hits, pre_grad).astype(BF)
    ext_grad = back(kept, w_one, WIDE)
    own_grad[...] = ext_grad[:sites]
    to_above, to_below = ext_grad[sites + rim : sites + 2 * rim], ext_grad[rims]
    near_pick = face_sites(near_row, sites).T.astype(BF)
    far_pick = face_sites(far_row, sites).T.astype(BF)
    to_near = jnp.where(above, to_above, to_below)
    coarse = to_near.astype(BF)
    theirs[offsets, :rim] = dot(near_pick, hidden.astype(BF)).astype(BF)
    theirs[offsets, rim : 2 * rim] = coarse
    theirs[offsets, 2 * rim : 3 * rim] = (to_near - coarse.astype(F32)).astype(BF)
    theirs[offsets, 3 * rim :] = jnp.zeros((channels - 3 * rim, channels), BF)
    far_out[:rim] = dot(far_pick, hidden.astype(BF))
    far_out[rim:] = jnp.where(above, to_below, to_above)
    first_is_mine = lax.axis_index("core") == 0
    for k in range(0, offsets, 2):
        n = min(2, offsets - k)
        first = dot(extended_t, kept[:, lanes(k, channels, n)])
        second = dot(hidden_t, held[:, lanes(k, channels, n)])
        for j in range(n):
            a, b = first[:, lanes(j, channels)], second[:, lanes(j, channels)]
            mine[k + j] = jnp.where(first_is_mine, a, b).astype(BF)
            theirs[k + j] = jnp.where(first_is_mine, b, a).astype(BF)
    mine[offsets] = jnp.zeros((channels, channels), BF)


def last_kernel(
    counts, hidden, faces, near, far, own_grad, picks, w_two,
    response, input_grad, picked, sems,
):
    sites, rim = hidden.shape[0], faces.shape[1]
    offsets, channels = w_two.shape[0], w_two.shape[1]
    live = live_rows(counts, sites)
    above = near_is_above()
    near_row, far_row = near_and_far(faces[0:1], faces[1:2])
    near_grad = near[rim : 2 * rim].astype(F32) + near[2 * rim : 3 * rim].astype(F32)
    grad = own_grad[...] + dot(face_sites(near_row, sites), near_grad, exact=True)
    grad = grad + dot(face_sites(far_row, sites), far[rim:], exact=True)
    input_grad[...] = jnp.where(live, grad, 0.0).astype(BF)
    near_rim = near[:rim].astype(F32)
    extended = extend(
        hidden[...].astype(F32),
        jnp.where(above, far[:rim], near_rim),
        jnp.where(above, near_rim, far[:rim]),
    )
    for k in range(offsets):
        picked[:, lanes(k, channels)] = dot(picks[k], extended).astype(BF)
    second_pre = dot(picked[...], w_two[...].reshape(offsets * channels, channels))
    response[...] = jnp.where(live, second_pre, 0.0).astype(BF)


def call(kernel, places, outs, scratch, copies, us, limit=16):
    spec = {
        "s": pl.BlockSpec(memory_space=pltpu.SMEM),
        "v": pl.BlockSpec(memory_space=pltpu.VMEM),
        "h": pl.BlockSpec(memory_space=pltpu.HBM),
    }
    return pl.pallas_call(
        kernel,
        out_shape=[jax.ShapeDtypeStruct(s, d) for s, d in outs],
        in_specs=[spec[p] for p in places],
        out_specs=[pl.BlockSpec(memory_space=pltpu.VMEM)] * len(outs),
        scratch_shapes=[pltpu.VMEM(s, d) for s, d in scratch]
        + [pltpu.SemaphoreType.DMA((copies,))],
        compiler_params=pltpu.CompilerParams(vmem_limit_bytes=limit * 2**20),
        cost_estimate=pl.CostEstimate(
            flops=0, bytes_accessed=int(us * 3e6), transcendentals=0
        ),
    )


def far_slab(block):
    last = lax.axis_size(SLAB) - 1
    pairs = [p for i in range(1, last, 2) for p in ((i, i + 1), (i + 1, i))]
    return lax.ppermute(block, SLAB, pairs)


def swap(block, axis):
    return lax.all_to_all(block, axis, 0, 0, tiled=True)


def other_core(block):
    return lax.ppermute(block, "core", [(0, 1), (1, 0)])


def on_device(feat, counts, nb, low, high, w_one, w_two, cot):
    sites, channels = feat.shape
    offsets, rim = nb.shape[1], low.shape[0]
    scaling = 1.0 / math.sqrt(lax.axis_size(AXES) * sites)
    flat = ((sites, channels), BF)
    field = ((sites, channels), F32)
    message = ((sites + 2 * rim, channels), BF)
    ends = ((2 * rim, channels), F32)
    weight = ((offsets, channels, channels), BF)
    sums = ((offsets + 1, channels, channels), BF)
    row = ((1, rim), jnp.int32)
    faces = ((2, rim), F32)
    picks = ((offsets, sites, WIDE), BF)
    broad = ((sites, offsets * channels), BF)
    low, high, table = low.reshape(1, rim), high.reshape(1, rim), nb.T
    letters = call(
        pack_kernel, "shhhhh", (message, message, faces),
        (flat, flat, ((offsets, sites), jnp.int32), row, row), 5, 1, limit=60,
    )(counts, feat, cot, table, low, high)
    masked, grad, names, faces, picks, w_one, w_two = call(
        stage_kernel, "svvvvv",
        (flat, flat, ((rim, sites), F32), faces, picks, weight, weight), (), 1, 2,
    )(counts, feat, letters[1], letters[2], w_one, w_two)
    near, far = other_core(letters[0]), far_slab(letters[1])
    far_two, own_grad, hidden, mine, theirs = call(
        main_kernel, "svvvvvvvvv", (ends, field, flat, sums, sums),
        (broad, broad, ((WIDE, offsets * channels), BF)), 1, 5,
    )(counts, masked, grad, names, faces, picks, w_one, w_two, far, near)

    depth, plane = lax.axis_size(DEPTH), lax.axis_size(PLANE)
    near = other_core(theirs)
    share = (mine.astype(F32) + near.astype(F32)).astype(BF)
    parts = swap(share.reshape(plane, -1, channels), PLANE)
    parts = jnp.sum(parts.astype(F32), 0).reshape(depth, -1, channels)
    total = jnp.sum(swap(parts, DEPTH), 0) * scaling

    total = total.astype(BF)
    column = swap(jnp.broadcast_to(total, (depth, *total.shape)), DEPTH)
    column = column.reshape(-1, channels)
    column, far_two = lax.optimization_barrier((column, far_two))
    whole = swap(jnp.broadcast_to(column, (plane, *column.shape)), PLANE)
    whole, far = lax.optimization_barrier((whole, far_slab(far_two)))
    whole = whole.reshape(offsets + 1, channels, channels)
    other = other_core(whole)
    response, input_grad = call(
        last_kernel, "svvvvvvv", (flat, flat), (broad,), 1, 3
    )(counts, hidden, faces, near[offsets], far, own_grad, picks, w_two)
    first_is_mine = lax.axis_index("core") == 0
    first = jnp.where(first_is_mine, whole, other)[:offsets]
    second = jnp.where(first_is_mine, other, whole)[:offsets]
    return response, input_grad, first, second


def solution(mesh):
    groups, slabs = mesh.devices.shape
    side = {64: 4, 16: 2, 4: 1}[slabs]
    fine = Mesh(mesh.devices.reshape(groups, side, side, 2, 2), AXES)
    rows, row = P(AXES, None), P(AXES)
    return jax.shard_map(
        on_device,
        mesh=fine,
        in_specs=(rows, row, rows, row, row, P(), P(), rows),
        out_specs=(rows, rows, P(), P()),
        check_vma=False,
    )
```

```python
import math

import jax
import jax.numpy as jnp
from jax import lax
from jax.experimental import pallas as pl
from jax.experimental.pallas import tpu as pltpu
from jax.sharding import Mesh, PartitionSpec as P

AXES = ("column", "pair", "y", "x", "zh", "core")
SLAB = ("y", "x", "zh", "core")
BLOCK = ("pair", "y", "x")
COLUMN = ("column", "zh")
BF = jnp.bfloat16
F32 = jnp.float32
WIDE = 256
NOWHERE = 255.0


def dot(a, b, contract=(1, 0), exact=False):
    return lax.dot_general(
        a,
        b,
        (((contract[0],), (contract[1],)), ((), ())),
        preferred_element_type=F32,
        precision=lax.Precision.HIGHEST if exact else None,
    )


def iota(shape, dim):
    return lax.broadcasted_iota(jnp.int32, shape, dim).astype(F32)


def live_rows(counts_ref, sites):
    return lax.broadcasted_iota(jnp.int32, (sites, 1), 0) < counts_ref[0]


def face_sites(row, sites):
    return (iota((sites, row.shape[1]), 0) == row).astype(F32)


def pick_matrix(columns, k):
    sites = columns.shape[0]
    return jnp.where(iota((sites, WIDE), 1) == columns[:, k : k + 1], 1.0, 0.0).astype(BF)


def gather_conv(extended, picks, w_ref):
    total = jnp.zeros((w_ref.shape[1], w_ref.shape[2]), F32)
    for k in range(w_ref.shape[0]):
        total = total + dot(dot(picks(k), extended).astype(BF), w_ref[k])
    return total


def extend(values, below, above):
    rim = below.shape[0]
    pad = jnp.zeros((WIDE - values.shape[0] - 2 * rim, values.shape[1]), F32)
    return jnp.concatenate([values, below, above, pad], 0).astype(BF)


def fetch(sources, targets, sems):
    copies = [
        pltpu.make_async_copy(s, t, sems.at[i])
        for i, (s, t) in enumerate(zip(sources, targets))
    ]
    for copy in copies:
        copy.start()
    return copies


def near_is_above():
    return lax.axis_index("core") == 0


def near_and_far(low, high):
    above = near_is_above()
    return jnp.where(above, high, low), jnp.where(above, low, high)


def pack_kernel(
    counts, feat_h, cot_h, map_h, low_h, high_h, near, far, faces,
    feat, cot, table, low, high, sems,
):
    for copy in fetch(
        (feat_h, cot_h, map_h, low_h, high_h), (feat, cot, table, low, high), sems
    ):
        copy.wait()
    live = live_rows(counts, feat.shape[0])
    faces[0:1] = low[...].astype(F32)
    faces[1:2] = high[...].astype(F32)
    offsets, sites = table.shape
    rim = low.shape[1]
    masked = jnp.where(live, feat[...].astype(F32), 0.0).astype(BF)
    grad = jnp.where(live, cot[...].astype(F32), 0.0).astype(BF)
    blank = jnp.full((rim - offsets, sites), NOWHERE, F32)
    names = jnp.concatenate([table[...].astype(F32), blank], 0).astype(BF)
    for out, row in zip((far, near), near_and_far(faces[1:2], faces[0:1])):
        out[:sites] = grad
        picks = face_sites(row, sites).T.astype(BF)
        out[sites : sites + rim] = dot(picks, masked).astype(BF)
        out[sites + rim :] = names


def stage_kernel(
    counts, feat, own, sides, w_one_in, w_two_in,
    masked, grad, names, faces, picks, w_one, w_two, sems,
):
    sites, rim = feat.shape[0], sides.shape[1]
    live = live_rows(counts, sites)
    masked[...] = jnp.where(live, feat[...].astype(F32), 0.0).astype(BF)
    grad[...] = own[:sites]
    names[...] = own[sites + rim :].astype(F32)
    faces[...] = sides[...]
    columns = names[...].T
    for k in range(picks.shape[0]):
        picks[k] = pick_matrix(columns, k)
        w_one[k] = w_one_in[k]
        w_two[k] = w_two_in[k]


def sites_of(names, first, row):
    found = jnp.full(names.shape, NOWHERE, F32)
    for j in range(row.shape[1]):
        found = jnp.where(names == first + j, row[:, j : j + 1], found)
    return found


def lanes(k, width, n=1):
    return slice(k * width, (k + n) * width)


def back(held, w_ref, rows):
    offsets, channels = w_ref.shape[0], w_ref.shape[1]
    total = jnp.zeros((rows, channels), F32)
    for k in range(0, offsets, 2):
        n = min(2, offsets - k)
        weight = jnp.concatenate([w_ref[k + j] for j in range(n)], 1)
        total = total + dot(held[:, lanes(k, w_ref.shape[2], n)], weight, (1, 1))
    return total


def main_kernel(
    counts, masked, own_grads, own_names, faces, picks, w_one, w_two, far, near,
    far_out, own_grad, hidden_ref, mine, theirs,
    picked, held, kept, sems,
):
    offsets, channels = w_one.shape[0], w_one.shape[1]
    sites, rim = masked.shape[0], faces.shape[1]
    live = live_rows(counts, sites)
    above = near_is_above()
    near_row, far_row = near_and_far(faces[0:1], faces[1:2])
    rims = slice(sites, sites + rim)
    near_rim, far_rim = near[rims].astype(F32), far[rims].astype(F32)
    extended = extend(
        masked[...].astype(F32),
        jnp.where(above, far_rim, near_rim),
        jnp.where(above, near_rim, far_rim),
    )
    for k in range(offsets):
        picked[:, lanes(k, channels)] = dot(picks[k], extended).astype(BF)
    x = dot(picked[...], w_one[...].reshape(offsets * channels, channels))

    up_first, down_first = float(sites), float(sites + rim)
    near_first = jnp.where(above, up_first, down_first)
    far_first = jnp.where(above, down_first, up_first)
    names = jnp.concatenate(
        [
            own_names[...],
            sites_of(near[sites + rim :].astype(F32), near_first, near_row),
            sites_of(far[sites + rim :].astype(F32), far_first, far_row),
        ],
        1,
    )
    grads = jnp.concatenate([own_grads[...], near[:sites], far[:sites]], 0)
    rows = iota((sites, 3 * sites), 0)
    for k in range(offsets):
        hits = jnp.where(rows == names[k : k + 1], 1.0, 0.0).astype(BF)
        held[:, lanes(k, channels)] = dot(hits, grads).astype(BF)
    hidden_grad = back(held, w_two, sites)

    slope = math.sqrt(2.0 / math.pi)
    t = jnp.tanh(slope * (x + 0.044715 * (x * x * x)))
    cdf = 0.5 * (1.0 + t)
    hidden = jnp.where(live, x * cdf, 0.0)
    hidden_ref[...] = hidden.astype(BF)
    bend = cdf + 0.5 * x * (1.0 - t * t) * (slope * (1.0 + 3 * 0.044715 * (x * x)))
    pre_grad = jnp.where(live, bend * hidden_grad, 0.0).astype(BF)

    extended_t = extended.astype(F32).T.astype(BF)
    hidden_t = hidden.T.astype(BF)
    rows = iota((WIDE, sites), 0)
    for k in range(offsets):
        hits = jnp.where(rows == names[k : k + 1, :sites], 1.0, 0.0).astype(BF)
        kept[:, lanes(k, channels)] = dot(hits, pre_grad).astype(BF)
    ext_grad = back(kept, w_one, WIDE)
    own_grad[...] = ext_grad[:sites]
    to_above, to_below = ext_grad[sites + rim : sites + 2 * rim], ext_grad[rims]
    near_pick = face_sites(near_row, sites).T.astype(BF)
    far_pick = face_sites(far_row, sites).T.astype(BF)
    to_near = jnp.where(above, to_above, to_below)
    coarse = to_near.astype(BF)
    theirs[offsets, :rim] = dot(near_pick, hidden.astype(BF)).astype(BF)
    theirs[offsets, rim : 2 * rim] = coarse
    theirs[offsets, 2 * rim : 3 * rim] = (to_near - coarse.astype(F32)).astype(BF)
    theirs[offsets, 3 * rim :] = jnp.zeros((channels - 3 * rim, channels), BF)
    far_out[:rim] = dot(far_pick, hidden.astype(BF))
    far_out[rim:] = jnp.where(above, to_below, to_above)
    first_is_mine = lax.axis_index("core") == 0
    for k in range(0, offsets, 2):
        n = min(2, offsets - k)
        first = dot(extended_t, kept[:, lanes(k, channels, n)])
        second = dot(hidden_t, held[:, lanes(k, channels, n)])
        for j in range(n):
            a, b = first[:, lanes(j, channels)], second[:, lanes(j, channels)]
            mine[k + j] = jnp.where(first_is_mine, a, b).astype(BF)
            theirs[k + j] = jnp.where(first_is_mine, b, a).astype(BF)
    mine[offsets] = jnp.zeros((channels, channels), BF)


def last_kernel(
    counts, hidden, faces, near, far, own_grad, picks, w_two,
    response, input_grad, picked, sems,
):
    sites, rim = hidden.shape[0], faces.shape[1]
    offsets, channels = w_two.shape[0], w_two.shape[1]
    live = live_rows(counts, sites)
    above = near_is_above()
    near_row, far_row = near_and_far(faces[0:1], faces[1:2])
    near_grad = near[rim : 2 * rim].astype(F32) + near[2 * rim : 3 * rim].astype(F32)
    grad = own_grad[...] + dot(face_sites(near_row, sites), near_grad, exact=True)
    grad = grad + dot(face_sites(far_row, sites), far[rim:], exact=True)
    input_grad[...] = jnp.where(live, grad, 0.0).astype(BF)
    near_rim = near[:rim].astype(F32)
    extended = extend(
        hidden[...].astype(F32),
        jnp.where(above, far[:rim], near_rim),
        jnp.where(above, near_rim, far[:rim]),
    )
    for k in range(offsets):
        picked[:, lanes(k, channels)] = dot(picks[k], extended).astype(BF)
    second_pre = dot(picked[...], w_two[...].reshape(offsets * channels, channels))
    response[...] = jnp.where(live, second_pre, 0.0).astype(BF)


def call(kernel, places, outs, scratch, copies, us, limit=16):
    spec = {
        "s": pl.BlockSpec(memory_space=pltpu.SMEM),
        "v": pl.BlockSpec(memory_space=pltpu.VMEM),
        "h": pl.BlockSpec(memory_space=pltpu.HBM),
    }
    return pl.pallas_call(
        kernel,
        out_shape=[jax.ShapeDtypeStruct(s, d) for s, d in outs],
        in_specs=[spec[p] for p in places],
        out_specs=[pl.BlockSpec(memory_space=pltpu.VMEM)] * len(outs),
        scratch_shapes=[pltpu.VMEM(s, d) for s, d in scratch]
        + [pltpu.SemaphoreType.DMA((copies,))],
        compiler_params=pltpu.CompilerParams(vmem_limit_bytes=limit * 2**20),
        cost_estimate=pl.CostEstimate(
            flops=0, bytes_accessed=int(us * 3e6), transcendentals=0
        ),
    )


def far_slab(block):
    last = lax.axis_size(SLAB) - 1
    pairs = [p for i in range(1, last, 2) for p in ((i, i + 1), (i + 1, i))]
    return lax.ppermute(block, SLAB, pairs)


def swap(block, axis):
    return lax.all_to_all(block, axis, 0, 0, tiled=True)


def other_core(block):
    return lax.ppermute(block, "core", [(0, 1), (1, 0)])


def on_device(feat, counts, nb, low, high, w_one, w_two, cot):
    sites, channels = feat.shape
    offsets, rim = nb.shape[1], low.shape[0]
    scaling = 1.0 / math.sqrt(lax.axis_size(AXES) * sites)
    half = math.sqrt(scaling)
    flat = ((sites, channels), BF)
    field = ((sites, channels), F32)
    message = ((sites + 2 * rim, channels), BF)
    ends = ((2 * rim, channels), F32)
    weight = ((offsets, channels, channels), BF)
    sums = ((offsets + 1, channels, channels), BF)
    row = ((1, rim), jnp.int32)
    faces = ((2, rim), F32)
    picks = ((offsets, sites, WIDE), BF)
    broad = ((sites, offsets * channels), BF)
    low, high, table = low.reshape(1, rim), high.reshape(1, rim), nb.T
    letters = call(
        pack_kernel, "shhhhh", (message, message, faces),
        (flat, flat, ((offsets, sites), jnp.int32), row, row), 5, 1, limit=60,
    )(counts, feat, cot, table, low, high)
    masked, grad, names, faces, picks, w_one, w_two = call(
        stage_kernel, "svvvvv",
        (flat, flat, ((rim, sites), F32), faces, picks, weight, weight), (), 1, 2,
    )(counts, feat, letters[1], letters[2], w_one, w_two)
    near, far = other_core(letters[0]), far_slab(letters[1])
    far_two, own_grad, hidden, mine, theirs = call(
        main_kernel, "svvvvvvvvv", (ends, field, flat, sums, sums),
        (broad, broad, ((WIDE, offsets * channels), BF)), 1, 5,
    )(counts, masked, grad, names, faces, picks, w_one, w_two, far, near)

    column, block = lax.axis_size(COLUMN), lax.axis_size(BLOCK)
    near = other_core(theirs)
    share = (mine.astype(F32) + near.astype(F32)).astype(BF)
    share, far_two = lax.optimization_barrier((share, far_two))
    parts = swap(share.reshape(block, -1, channels), BLOCK)
    far = far_slab(far_two)
    parts = (jnp.sum(parts.astype(F32), 0) * half).astype(BF)
    parts, far = lax.optimization_barrier((parts, far))
    parts = swap(jnp.broadcast_to(parts, (column, *parts.shape)), COLUMN)
    response, input_grad = call(
        last_kernel, "svvvvvvv", (flat, flat), (broad,), 1, 3
    )(counts, hidden, faces, near[offsets], far, own_grad, picks, w_two)
    total = (jnp.sum(parts.astype(F32), 0) * half).astype(BF)
    total, response, input_grad = lax.optimization_barrier((total, response, input_grad))

    whole = swap(jnp.broadcast_to(total, (block, *total.shape)), BLOCK)
    whole = whole.reshape(offsets + 1, channels, channels)
    other = other_core(whole)
    first_is_mine = lax.axis_index("core") == 0
    first = jnp.where(first_is_mine, whole, other)[:offsets]
    second = jnp.where(first_is_mine, other, whole)[:offsets]
    return response, input_grad, first, second


def solution(mesh):
    groups, slabs = mesh.devices.shape
    side = {64: 4, 16: 2, 4: 1}[slabs]
    pair = 2 if groups % 2 == 0 else 1
    fine = Mesh(mesh.devices.reshape(groups // pair, pair, side, side, 2, 2), AXES)
    rows, row = P(AXES, None), P(AXES)
    return jax.shard_map(
        on_device,
        mesh=fine,
        in_specs=(rows, row, rows, row, row, P(), P(), rows),
        out_specs=(rows, rows, P(), P()),
        check_vma=False,
    )
```

```python
import math

import jax
import jax.numpy as jnp
from jax import lax
from jax.experimental import pallas as pl
from jax.experimental.pallas import tpu as pltpu
from jax.sharding import Mesh, PartitionSpec as P

AXES = ("column", "pair", "y", "x", "zh", "core")
SLAB = ("y", "x", "zh", "core")
BLOCK = ("pair", "y", "x")
COLUMN = ("column", "zh")
BF = jnp.bfloat16
F32 = jnp.float32
WIDE = 256
NOWHERE = 255.0


def dot(a, b, contract=(1, 0), exact=False):
    return lax.dot_general(
        a,
        b,
        (((contract[0],), (contract[1],)), ((), ())),
        preferred_element_type=F32,
        precision=lax.Precision.HIGHEST if exact else None,
    )


def iota(shape, dim):
    return lax.broadcasted_iota(jnp.int32, shape, dim).astype(F32)


def live_rows(counts_ref, sites):
    return lax.broadcasted_iota(jnp.int32, (sites, 1), 0) < counts_ref[0]


def face_sites(row, sites):
    return (iota((sites, row.shape[1]), 0) == row).astype(F32)


def pick_matrix(columns, k):
    sites = columns.shape[0]
    return jnp.where(iota((sites, WIDE), 1) == columns[:, k : k + 1], 1.0, 0.0).astype(BF)


def gather_conv(extended, picks, w_ref):
    total = jnp.zeros((w_ref.shape[1], w_ref.shape[2]), F32)
    for k in range(w_ref.shape[0]):
        total = total + dot(dot(picks(k), extended).astype(BF), w_ref[k])
    return total


def extend(values, below, above):
    rim = below.shape[0]
    pad = jnp.zeros((WIDE - values.shape[0] - 2 * rim, values.shape[1]), F32)
    return jnp.concatenate([values, below, above, pad], 0).astype(BF)


def fetch(sources, targets, sems):
    copies = [
        pltpu.make_async_copy(s, t, sems.at[i])
        for i, (s, t) in enumerate(zip(sources, targets))
    ]
    for copy in copies:
        copy.start()
    return copies


def near_is_above():
    return lax.axis_index("core") == 0


def near_and_far(low, high):
    above = near_is_above()
    return jnp.where(above, high, low), jnp.where(above, low, high)


def pack_kernel(
    counts, feat_h, cot_h, map_h, low_h, high_h, near, far, faces,
    feat, cot, table, low, high, sems,
):
    for copy in fetch(
        (feat_h, cot_h, map_h, low_h, high_h), (feat, cot, table, low, high), sems
    ):
        copy.wait()
    live = live_rows(counts, feat.shape[0])
    faces[0:1] = low[...].astype(F32)
    faces[1:2] = high[...].astype(F32)
    offsets, sites = table.shape
    rim = low.shape[1]
    masked = jnp.where(live, feat[...].astype(F32), 0.0).astype(BF)
    grad = jnp.where(live, cot[...].astype(F32), 0.0).astype(BF)
    blank = jnp.full((rim - offsets, sites), NOWHERE, F32)
    names = jnp.concatenate([table[...].astype(F32), blank], 0).astype(BF)
    for out, row in zip((far, near), near_and_far(faces[1:2], faces[0:1])):
        out[:sites] = grad
        picks = face_sites(row, sites).T.astype(BF)
        out[sites : sites + rim] = dot(picks, masked).astype(BF)
        out[sites + rim :] = names


def stage_kernel(
    counts, feat, own, sides, w_one_in, w_two_in,
    masked, grad, names, faces, picks, w_one, w_two, sems,
):
    sites, rim = feat.shape[0], sides.shape[1]
    live = live_rows(counts, sites)
    masked[...] = jnp.where(live, feat[...].astype(F32), 0.0).astype(BF)
    grad[...] = own[:sites]
    names[...] = own[sites + rim :].astype(F32)
    faces[...] = sides[...]
    columns = names[...].T
    for k in range(picks.shape[0]):
        picks[k] = pick_matrix(columns, k)
        w_one[k] = w_one_in[k]
        w_two[k] = w_two_in[k]


def sites_of(names, first, row):
    found = jnp.full(names.shape, NOWHERE, F32)
    for j in range(row.shape[1]):
        found = jnp.where(names == first + j, row[:, j : j + 1], found)
    return found


def lanes(k, width, n=1):
    return slice(k * width, (k + n) * width)


def back(held, w_ref, rows):
    offsets, channels = w_ref.shape[0], w_ref.shape[1]
    total = jnp.zeros((rows, channels), F32)
    for k in range(0, offsets, 2):
        n = min(2, offsets - k)
        weight = jnp.concatenate([w_ref[k + j] for j in range(n)], 1)
        total = total + dot(held[:, lanes(k, w_ref.shape[2], n)], weight, (1, 1))
    return total


def main_kernel(
    counts, masked, own_grads, own_names, faces, picks, w_one, w_two, far, near,
    far_out, own_grad, hidden_ref, mine, theirs,
    picked, held, kept, sems,
):
    offsets, channels = w_one.shape[0], w_one.shape[1]
    sites, rim = masked.shape[0], faces.shape[1]
    live = live_rows(counts, sites)
    above = near_is_above()
    near_row, far_row = near_and_far(faces[0:1], faces[1:2])
    rims = slice(sites, sites + rim)
    near_rim, far_rim = near[rims].astype(F32), far[rims].astype(F32)
    extended = extend(
        masked[...].astype(F32),
        jnp.where(above, far_rim, near_rim),
        jnp.where(above, near_rim, far_rim),
    )
    for k in range(offsets):
        picked[:, lanes(k, channels)] = dot(picks[k], extended).astype(BF)
    x = dot(picked[...], w_one[...].reshape(offsets * channels, channels))

    up_first, down_first = float(sites), float(sites + rim)
    near_first = jnp.where(above, up_first, down_first)
    far_first = jnp.where(above, down_first, up_first)
    names = jnp.concatenate(
        [
            own_names[...],
            sites_of(near[sites + rim :].astype(F32), near_first, near_row),
            sites_of(far[sites + rim :].astype(F32), far_first, far_row),
        ],
        1,
    )
    grads = jnp.concatenate([own_grads[...], near[:sites], far[:sites]], 0)
    rows = iota((sites, 3 * sites), 0)
    for k in range(offsets):
        hits = jnp.where(rows == names[k : k + 1], 1.0, 0.0).astype(BF)
        held[:, lanes(k, channels)] = dot(hits, grads).astype(BF)
    hidden_grad = back(held, w_two, sites)

    slope = math.sqrt(2.0 / math.pi)
    t = jnp.tanh(slope * (x + 0.044715 * (x * x * x)))
    cdf = 0.5 * (1.0 + t)
    hidden = jnp.where(live, x * cdf, 0.0)
    hidden_ref[...] = hidden.astype(BF)
    bend = cdf + 0.5 * x * (1.0 - t * t) * (slope * (1.0 + 3 * 0.044715 * (x * x)))
    pre_grad = jnp.where(live, bend * hidden_grad, 0.0).astype(BF)

    extended_t = extended.astype(F32).T.astype(BF)
    hidden_t = hidden.T.astype(BF)
    rows = iota((WIDE, sites), 0)
    for k in range(offsets):
        hits = jnp.where(rows == names[k : k + 1, :sites], 1.0, 0.0).astype(BF)
        kept[:, lanes(k, channels)] = dot(hits, pre_grad).astype(BF)
    ext_grad = back(kept, w_one, WIDE)
    own_grad[...] = ext_grad[:sites]
    to_above, to_below = ext_grad[sites + rim : sites + 2 * rim], ext_grad[rims]
    near_pick = face_sites(near_row, sites).T.astype(BF)
    far_pick = face_sites(far_row, sites).T.astype(BF)
    to_near = jnp.where(above, to_above, to_below)
    coarse = to_near.astype(BF)
    theirs[offsets, :rim] = dot(near_pick, hidden.astype(BF)).astype(BF)
    theirs[offsets, rim : 2 * rim] = coarse
    theirs[offsets, 2 * rim : 3 * rim] = (to_near - coarse.astype(F32)).astype(BF)
    theirs[offsets, 3 * rim :] = jnp.zeros((channels - 3 * rim, channels), BF)
    far_out[:rim] = dot(far_pick, hidden.astype(BF))
    far_out[rim:] = jnp.where(above, to_below, to_above)
    first_is_mine = lax.axis_index("core") == 0
    for k in range(0, offsets, 2):
        n = min(2, offsets - k)
        first = dot(extended_t, kept[:, lanes(k, channels, n)])
        second = dot(hidden_t, held[:, lanes(k, channels, n)])
        for j in range(n):
            a, b = first[:, lanes(j, channels)], second[:, lanes(j, channels)]
            mine[k + j] = jnp.where(first_is_mine, a, b).astype(BF)
            theirs[k + j] = jnp.where(first_is_mine, b, a).astype(BF)
    mine[offsets] = jnp.zeros((channels, channels), BF)


def last_kernel(
    counts, hidden, faces, near, far, own_grad, picks, w_two,
    response, input_grad, picked, sems,
):
    sites, rim = hidden.shape[0], faces.shape[1]
    offsets, channels = w_two.shape[0], w_two.shape[1]
    live = live_rows(counts, sites)
    above = near_is_above()
    near_row, far_row = near_and_far(faces[0:1], faces[1:2])
    near_grad = near[rim : 2 * rim].astype(F32) + near[2 * rim : 3 * rim].astype(F32)
    grad = own_grad[...] + dot(face_sites(near_row, sites), near_grad, exact=True)
    grad = grad + dot(face_sites(far_row, sites), far[rim:], exact=True)
    input_grad[...] = jnp.where(live, grad, 0.0).astype(BF)
    near_rim = near[:rim].astype(F32)
    extended = extend(
        hidden[...].astype(F32),
        jnp.where(above, far[:rim], near_rim),
        jnp.where(above, near_rim, far[:rim]),
    )
    for k in range(offsets):
        picked[:, lanes(k, channels)] = dot(picks[k], extended).astype(BF)
    second_pre = dot(picked[...], w_two[...].reshape(offsets * channels, channels))
    response[...] = jnp.where(live, second_pre, 0.0).astype(BF)


def call(kernel, places, outs, scratch, copies, us, limit=16):
    spec = {
        "s": pl.BlockSpec(memory_space=pltpu.SMEM),
        "v": pl.BlockSpec(memory_space=pltpu.VMEM),
        "h": pl.BlockSpec(memory_space=pltpu.HBM),
    }
    return pl.pallas_call(
        kernel,
        out_shape=[jax.ShapeDtypeStruct(s, d) for s, d in outs],
        in_specs=[spec[p] for p in places],
        out_specs=[pl.BlockSpec(memory_space=pltpu.VMEM)] * len(outs),
        scratch_shapes=[pltpu.VMEM(s, d) for s, d in scratch]
        + [pltpu.SemaphoreType.DMA((copies,))],
        compiler_params=pltpu.CompilerParams(vmem_limit_bytes=limit * 2**20),
        cost_estimate=pl.CostEstimate(
            flops=0, bytes_accessed=int(us * 3e6), transcendentals=0
        ),
    )


def far_slab(block):
    last = lax.axis_size(SLAB) - 1
    pairs = [p for i in range(1, last, 2) for p in ((i, i + 1), (i + 1, i))]
    return lax.ppermute(block, SLAB, pairs)


def swap(block, axis):
    return lax.all_to_all(block, axis, 0, 0, tiled=True)


def other_core(block):
    return lax.ppermute(block, "core", [(0, 1), (1, 0)])


def on_device(feat, counts, nb, low, high, w_one, w_two, cot):
    sites, channels = feat.shape
    offsets, rim = nb.shape[1], low.shape[0]
    scaling = 1.0 / math.sqrt(lax.axis_size(AXES) * sites)
    half = math.sqrt(scaling)
    flat = ((sites, channels), BF)
    field = ((sites, channels), F32)
    message = ((sites + 2 * rim, channels), BF)
    ends = ((2 * rim, channels), F32)
    weight = ((offsets, channels, channels), BF)
    sums = ((offsets + 1, channels, channels), BF)
    row = ((1, rim), jnp.int32)
    faces = ((2, rim), F32)
    picks = ((offsets, sites, WIDE), BF)
    broad = ((sites, offsets * channels), BF)
    low, high, table = low.reshape(1, rim), high.reshape(1, rim), nb.T
    letters = call(
        pack_kernel, "shhhhh", (message, message, faces),
        (flat, flat, ((offsets, sites), jnp.int32), row, row), 5, 1, limit=60,
    )(counts, feat, cot, table, low, high)
    masked, grad, names, faces, picks, w_one, w_two = call(
        stage_kernel, "svvvvv",
        (flat, flat, ((rim, sites), F32), faces, picks, weight, weight), (), 1, 2,
    )(counts, feat, letters[1], letters[2], w_one, w_two)
    near, far = other_core(letters[0]), far_slab(letters[1])
    far_two, own_grad, hidden, mine, theirs = call(
        main_kernel, "svvvvvvvvv", (ends, field, flat, sums, sums),
        (broad, broad, ((WIDE, offsets * channels), BF)), 1, 5,
    )(counts, masked, grad, names, faces, picks, w_one, w_two, far, near)

    column, block = lax.axis_size(COLUMN), lax.axis_size(BLOCK)
    near = other_core(theirs)
    share = (mine.astype(F32) + near.astype(F32)).astype(BF)
    parts = swap(share.reshape(block, -1, channels), BLOCK)
    parts = (jnp.sum(parts.astype(F32), 0) * half).astype(BF)
    parts, far_two = lax.optimization_barrier((parts, far_two))
    far = far_slab(far_two)
    parts = swap(jnp.broadcast_to(parts, (column, *parts.shape)), COLUMN)
    response, input_grad = call(
        last_kernel, "svvvvvvv", (flat, flat), (broad,), 1, 3
    )(counts, hidden, faces, near[offsets], far, own_grad, picks, w_two)
    total = (jnp.sum(parts.astype(F32), 0) * half).astype(BF)
    total, response, input_grad = lax.optimization_barrier((total, response, input_grad))

    whole = swap(jnp.broadcast_to(total, (block, *total.shape)), BLOCK)
    whole = whole.reshape(offsets + 1, channels, channels)
    other = other_core(whole)
    first_is_mine = lax.axis_index("core") == 0
    first = jnp.where(first_is_mine, whole, other)[:offsets]
    second = jnp.where(first_is_mine, other, whole)[:offsets]
    return response, input_grad, first, second


def solution(mesh):
    groups, slabs = mesh.devices.shape
    side = {64: 4, 16: 2, 4: 1}[slabs]
    pair = 2 if groups % 2 == 0 else 1
    fine = Mesh(mesh.devices.reshape(groups // pair, pair, side, side, 2, 2), AXES)
    rows, row = P(AXES, None), P(AXES)
    return jax.shard_map(
        on_device,
        mesh=fine,
        in_specs=(rows, row, rows, row, row, P(), P(), rows),
        out_specs=(rows, rows, P(), P()),
        check_vma=False,
    )
```

```python
import math

import jax
import jax.numpy as jnp
from jax import lax
from jax.experimental import pallas as pl
from jax.experimental.pallas import tpu as pltpu
from jax.sharding import Mesh, PartitionSpec as P

AXES = ("column", "pair", "y", "x", "zh", "core")
SLAB = ("y", "x", "zh", "core")
BLOCK = ("pair", "y", "x")
COLUMN = ("column", "zh")
BF = jnp.bfloat16
F32 = jnp.float32
WIDE = 256
NOWHERE = 255.0


def dot(a, b, contract=(1, 0), exact=False):
    return lax.dot_general(
        a,
        b,
        (((contract[0],), (contract[1],)), ((), ())),
        preferred_element_type=F32,
        precision=lax.Precision.HIGHEST if exact else None,
    )


def iota(shape, dim):
    return lax.broadcasted_iota(jnp.int32, shape, dim).astype(F32)


def live_rows(counts_ref, sites):
    return lax.broadcasted_iota(jnp.int32, (sites, 1), 0) < counts_ref[0]


def face_sites(row, sites):
    return (iota((sites, row.shape[1]), 0) == row).astype(F32)


def pick_matrix(columns, k):
    sites = columns.shape[0]
    return jnp.where(iota((sites, WIDE), 1) == columns[:, k : k + 1], 1.0, 0.0).astype(BF)


def gather_conv(extended, picks, w_ref):
    total = jnp.zeros((w_ref.shape[1], w_ref.shape[2]), F32)
    for k in range(w_ref.shape[0]):
        total = total + dot(dot(picks(k), extended).astype(BF), w_ref[k])
    return total


def extend(values, below, above):
    rim = below.shape[0]
    pad = jnp.zeros((WIDE - values.shape[0] - 2 * rim, values.shape[1]), F32)
    return jnp.concatenate([values, below, above, pad], 0).astype(BF)


def fetch(sources, targets, sems):
    copies = [
        pltpu.make_async_copy(s, t, sems.at[i])
        for i, (s, t) in enumerate(zip(sources, targets))
    ]
    for copy in copies:
        copy.start()
    return copies


def near_is_above():
    return lax.axis_index("core") == 0


def near_and_far(low, high):
    above = near_is_above()
    return jnp.where(above, high, low), jnp.where(above, low, high)


def pack_kernel(
    counts, feat_h, cot_h, map_h, low_h, high_h, near, far, faces,
    feat, cot, table, low, high, sems,
):
    for copy in fetch(
        (feat_h, cot_h, map_h, low_h, high_h), (feat, cot, table, low, high), sems
    ):
        copy.wait()
    live = live_rows(counts, feat.shape[0])
    faces[0:1] = low[...].astype(F32)
    faces[1:2] = high[...].astype(F32)
    offsets, sites = table.shape
    rim = low.shape[1]
    masked = jnp.where(live, feat[...].astype(F32), 0.0).astype(BF)
    grad = jnp.where(live, cot[...].astype(F32), 0.0).astype(BF)
    blank = jnp.full((rim - offsets, sites), NOWHERE, F32)
    names = jnp.concatenate([table[...].astype(F32), blank], 0).astype(BF)
    for out, row in zip((far, near), near_and_far(faces[1:2], faces[0:1])):
        out[:sites] = grad
        picks = face_sites(row, sites).T.astype(BF)
        out[sites : sites + rim] = dot(picks, masked).astype(BF)
        out[sites + rim :] = names


def stage_kernel(
    counts, feat, own, sides, w_one_in, w_two_in,
    masked, grad, names, faces, picks, w_one, w_two, sems,
):
    sites, rim = feat.shape[0], sides.shape[1]
    live = live_rows(counts, sites)
    masked[...] = jnp.where(live, feat[...].astype(F32), 0.0).astype(BF)
    grad[...] = own[:sites]
    names[...] = own[sites + rim :].astype(F32)
    faces[...] = sides[...]
    columns = names[...].T
    for k in range(picks.shape[0]):
        picks[k] = pick_matrix(columns, k)
        w_one[k] = w_one_in[k]
        w_two[k] = w_two_in[k]


def sites_of(names, first, row):
    found = jnp.full(names.shape, NOWHERE, F32)
    for j in range(row.shape[1]):
        found = jnp.where(names == first + j, row[:, j : j + 1], found)
    return found


def lanes(k, width, n=1):
    return slice(k * width, (k + n) * width)


def back(held, w_ref, rows):
    offsets, channels = w_ref.shape[0], w_ref.shape[1]
    total = jnp.zeros((rows, channels), F32)
    for k in range(0, offsets, 2):
        n = min(2, offsets - k)
        weight = jnp.concatenate([w_ref[k + j] for j in range(n)], 1)
        total = total + dot(held[:, lanes(k, w_ref.shape[2], n)], weight, (1, 1))
    return total


def main_kernel(
    counts, masked, own_grads, own_names, faces, picks, w_one, w_two, far, near,
    far_out, own_grad, hidden_ref, mine, theirs,
    picked, held, kept, sems,
):
    offsets, channels = w_one.shape[0], w_one.shape[1]
    sites, rim = masked.shape[0], faces.shape[1]
    live = live_rows(counts, sites)
    above = near_is_above()
    near_row, far_row = near_and_far(faces[0:1], faces[1:2])
    rims = slice(sites, sites + rim)
    near_rim, far_rim = near[rims].astype(F32), far[rims].astype(F32)
    extended = extend(
        masked[...].astype(F32),
        jnp.where(above, far_rim, near_rim),
        jnp.where(above, near_rim, far_rim),
    )
    for k in range(offsets):
        picked[:, lanes(k, channels)] = dot(picks[k], extended).astype(BF)
    x = dot(picked[...], w_one[...].reshape(offsets * channels, channels))

    up_first, down_first = float(sites), float(sites + rim)
    near_first = jnp.where(above, up_first, down_first)
    far_first = jnp.where(above, down_first, up_first)
    names = jnp.concatenate(
        [
            own_names[...],
            sites_of(near[sites + rim :].astype(F32), near_first, near_row),
            sites_of(far[sites + rim :].astype(F32), far_first, far_row),
        ],
        1,
    )
    grads = jnp.concatenate([own_grads[...], near[:sites], far[:sites]], 0)
    rows = iota((sites, 3 * sites), 0)
    for k in range(offsets):
        hits = jnp.where(rows == names[k : k + 1], 1.0, 0.0).astype(BF)
        held[:, lanes(k, channels)] = dot(hits, grads).astype(BF)
    hidden_grad = back(held, w_two, sites)

    slope = math.sqrt(2.0 / math.pi)
    t = jnp.tanh(slope * (x + 0.044715 * (x * x * x)))
    cdf = 0.5 * (1.0 + t)
    hidden = jnp.where(live, x * cdf, 0.0)
    hidden_ref[...] = hidden.astype(BF)
    bend = cdf + 0.5 * x * (1.0 - t * t) * (slope * (1.0 + 3 * 0.044715 * (x * x)))
    pre_grad = jnp.where(live, bend * hidden_grad, 0.0).astype(BF)

    extended_t = extended.astype(F32).T.astype(BF)
    hidden_t = hidden.T.astype(BF)
    rows = iota((WIDE, sites), 0)
    for k in range(offsets):
        hits = jnp.where(rows == names[k : k + 1, :sites], 1.0, 0.0).astype(BF)
        kept[:, lanes(k, channels)] = dot(hits, pre_grad).astype(BF)
    ext_grad = back(kept, w_one, WIDE)
    own_grad[...] = ext_grad[:sites]
    to_above, to_below = ext_grad[sites + rim : sites + 2 * rim], ext_grad[rims]
    near_pick = face_sites(near_row, sites).T.astype(BF)
    far_pick = face_sites(far_row, sites).T.astype(BF)
    to_near = jnp.where(above, to_above, to_below)
    coarse = to_near.astype(BF)
    theirs[offsets, :rim] = dot(near_pick, hidden.astype(BF)).astype(BF)
    theirs[offsets, rim : 2 * rim] = coarse
    theirs[offsets, 2 * rim : 3 * rim] = (to_near - coarse.astype(F32)).astype(BF)
    theirs[offsets, 3 * rim :] = jnp.zeros((channels - 3 * rim, channels), BF)
    far_out[:rim] = dot(far_pick, hidden.astype(BF))
    far_out[rim:] = jnp.where(above, to_below, to_above)
    first_is_mine = lax.axis_index("core") == 0
    for k in range(0, offsets, 2):
        n = min(2, offsets - k)
        first = dot(extended_t, kept[:, lanes(k, channels, n)])
        second = dot(hidden_t, held[:, lanes(k, channels, n)])
        for j in range(n):
            a, b = first[:, lanes(j, channels)], second[:, lanes(j, channels)]
            mine[k + j] = jnp.where(first_is_mine, a, b).astype(BF)
            theirs[k + j] = jnp.where(first_is_mine, b, a).astype(BF)
    mine[offsets] = jnp.zeros((channels, channels), BF)


def last_kernel(
    counts, hidden, faces, near, far, own_grad, picks, w_two,
    response, input_grad, picked, sems,
):
    sites, rim = hidden.shape[0], faces.shape[1]
    offsets, channels = w_two.shape[0], w_two.shape[1]
    live = live_rows(counts, sites)
    above = near_is_above()
    near_row, far_row = near_and_far(faces[0:1], faces[1:2])
    near_grad = near[rim : 2 * rim].astype(F32) + near[2 * rim : 3 * rim].astype(F32)
    grad = own_grad[...] + dot(face_sites(near_row, sites), near_grad, exact=True)
    grad = grad + dot(face_sites(far_row, sites), far[rim:], exact=True)
    input_grad[...] = jnp.where(live, grad, 0.0).astype(BF)
    near_rim = near[:rim].astype(F32)
    extended = extend(
        hidden[...].astype(F32),
        jnp.where(above, far[:rim], near_rim),
        jnp.where(above, near_rim, far[:rim]),
    )
    for k in range(offsets):
        picked[:, lanes(k, channels)] = dot(picks[k], extended).astype(BF)
    second_pre = dot(picked[...], w_two[...].reshape(offsets * channels, channels))
    response[...] = jnp.where(live, second_pre, 0.0).astype(BF)


def call(kernel, places, outs, scratch, copies, us, limit=16):
    spec = {
        "s": pl.BlockSpec(memory_space=pltpu.SMEM),
        "v": pl.BlockSpec(memory_space=pltpu.VMEM),
        "h": pl.BlockSpec(memory_space=pltpu.HBM),
    }
    return pl.pallas_call(
        kernel,
        out_shape=[jax.ShapeDtypeStruct(s, d) for s, d in outs],
        in_specs=[spec[p] for p in places],
        out_specs=[pl.BlockSpec(memory_space=pltpu.VMEM)] * len(outs),
        scratch_shapes=[pltpu.VMEM(s, d) for s, d in scratch]
        + [pltpu.SemaphoreType.DMA((copies,))],
        compiler_params=pltpu.CompilerParams(vmem_limit_bytes=limit * 2**20),
        cost_estimate=pl.CostEstimate(
            flops=0, bytes_accessed=int(us * 3e6), transcendentals=0
        ),
    )


def far_slab(block):
    last = lax.axis_size(SLAB) - 1
    pairs = [p for i in range(1, last, 2) for p in ((i, i + 1), (i + 1, i))]
    return lax.ppermute(block, SLAB, pairs)


def swap(block, axis):
    return lax.all_to_all(block, axis, 0, 0, tiled=True)


def other_core(block):
    return lax.ppermute(block, "core", [(0, 1), (1, 0)])


def on_device(feat, counts, nb, low, high, w_one, w_two, cot):
    sites, channels = feat.shape
    offsets, rim = nb.shape[1], low.shape[0]
    scaling = 1.0 / math.sqrt(lax.axis_size(AXES) * sites)
    half = math.sqrt(scaling)
    flat = ((sites, channels), BF)
    field = ((sites, channels), F32)
    message = ((sites + 2 * rim, channels), BF)
    ends = ((2 * rim, channels), F32)
    weight = ((offsets, channels, channels), BF)
    sums = ((offsets + 1, channels, channels), BF)
    row = ((1, rim), jnp.int32)
    faces = ((2, rim), F32)
    picks = ((offsets, sites, WIDE), BF)
    broad = ((sites, offsets * channels), BF)
    low, high, table = low.reshape(1, rim), high.reshape(1, rim), nb.T
    letters = call(
        pack_kernel, "shhhhh", (message, message, faces),
        (flat, flat, ((offsets, sites), jnp.int32), row, row), 5, 1, limit=60,
    )(counts, feat, cot, table, low, high)
    masked, grad, names, faces, picks, w_one, w_two = call(
        stage_kernel, "svvvvv",
        (flat, flat, ((rim, sites), F32), faces, picks, weight, weight), (), 1, 2,
    )(counts, feat, letters[1], letters[2], w_one, w_two)
    near, far = other_core(letters[0]), far_slab(letters[1])
    far_two, own_grad, hidden, mine, theirs = call(
        main_kernel, "svvvvvvvvv", (ends, field, flat, sums, sums),
        (broad, broad, ((WIDE, offsets * channels), BF)), 1, 5,
    )(counts, masked, grad, names, faces, picks, w_one, w_two, far, near)

    column, block = lax.axis_size(COLUMN), lax.axis_size(BLOCK)
    near = other_core(theirs)
    share = (mine.astype(F32) + near.astype(F32)).astype(BF)
    parts = swap(share.reshape(block, -1, channels), BLOCK)
    parts = (jnp.sum(parts.astype(F32), 0) * half).astype(BF)
    parts, far_two = lax.optimization_barrier((parts, far_two))
    far = far_slab(far_two)
    parts = swap(jnp.broadcast_to(parts, (column, *parts.shape)), COLUMN)
    total = (jnp.sum(parts.astype(F32), 0) * half).astype(BF)
    total, far = lax.optimization_barrier((total, far))
    response, input_grad = call(
        last_kernel, "svvvvvvv", (flat, flat), (broad,), 1, 3
    )(counts, hidden, faces, near[offsets], far, own_grad, picks, w_two)

    whole = swap(jnp.broadcast_to(total, (block, *total.shape)), BLOCK)
    whole, response, input_grad = lax.optimization_barrier((whole, response, input_grad))
    whole = whole.reshape(offsets + 1, channels, channels)
    other = other_core(whole)
    first_is_mine = lax.axis_index("core") == 0
    first = jnp.where(first_is_mine, whole, other)[:offsets]
    second = jnp.where(first_is_mine, other, whole)[:offsets]
    return response, input_grad, first, second


def solution(mesh):
    groups, slabs = mesh.devices.shape
    side = {64: 4, 16: 2, 4: 1}[slabs]
    pair = 2 if groups % 2 == 0 else 1
    fine = Mesh(mesh.devices.reshape(groups // pair, pair, side, side, 2, 2), AXES)
    rows, row = P(AXES, None), P(AXES)
    return jax.shard_map(
        on_device,
        mesh=fine,
        in_specs=(rows, row, rows, row, row, P(), P(), rows),
        out_specs=(rows, rows, P(), P()),
        check_vma=False,
    )
```

```python
import math

import jax
import jax.numpy as jnp
from jax import lax
from jax.experimental import pallas as pl
from jax.experimental.pallas import tpu as pltpu
from jax.sharding import Mesh, PartitionSpec as P

AXES = ("column", "pair", "y", "x", "zh", "core")
SLAB = ("y", "x", "zh", "core")
BLOCK = ("pair", "y", "x")
COLUMN = ("column", "zh")
BF = jnp.bfloat16
F32 = jnp.float32
WIDE = 256
NOWHERE = 255.0


def dot(a, b, contract=(1, 0), exact=False):
    return lax.dot_general(
        a,
        b,
        (((contract[0],), (contract[1],)), ((), ())),
        preferred_element_type=F32,
        precision=lax.Precision.HIGHEST if exact else None,
    )


def iota(shape, dim):
    return lax.broadcasted_iota(jnp.int32, shape, dim).astype(F32)


def live_rows(counts_ref, sites):
    return lax.broadcasted_iota(jnp.int32, (sites, 1), 0) < counts_ref[0]


def face_sites(row, sites):
    return (iota((sites, row.shape[1]), 0) == row).astype(F32)


def pick_matrix(columns, k):
    sites = columns.shape[0]
    return jnp.where(iota((sites, WIDE), 1) == columns[:, k : k + 1], 1.0, 0.0).astype(BF)


def gather_conv(extended, picks, w_ref):
    total = jnp.zeros((w_ref.shape[1], w_ref.shape[2]), F32)
    for k in range(w_ref.shape[0]):
        total = total + dot(dot(picks(k), extended).astype(BF), w_ref[k])
    return total


def extend(values, below, above):
    rim = below.shape[0]
    pad = jnp.zeros((WIDE - values.shape[0] - 2 * rim, values.shape[1]), F32)
    return jnp.concatenate([values, below, above, pad], 0).astype(BF)


def fetch(sources, targets, sems):
    copies = [
        pltpu.make_async_copy(s, t, sems.at[i])
        for i, (s, t) in enumerate(zip(sources, targets))
    ]
    for copy in copies:
        copy.start()
    return copies


def near_is_above():
    return lax.axis_index("core") == 0


def near_and_far(low, high):
    above = near_is_above()
    return jnp.where(above, high, low), jnp.where(above, low, high)


def pack_kernel(
    counts, feat_h, cot_h, map_h, low_h, high_h, near, far, faces,
    feat, cot, table, low, high, sems,
):
    for copy in fetch(
        (feat_h, cot_h, map_h, low_h, high_h), (feat, cot, table, low, high), sems
    ):
        copy.wait()
    live = live_rows(counts, feat.shape[0])
    faces[0:1] = low[...].astype(F32)
    faces[1:2] = high[...].astype(F32)
    offsets, sites = table.shape
    rim = low.shape[1]
    masked = jnp.where(live, feat[...].astype(F32), 0.0).astype(BF)
    grad = jnp.where(live, cot[...].astype(F32), 0.0).astype(BF)
    blank = jnp.full((rim - offsets, sites), NOWHERE, F32)
    names = jnp.concatenate([table[...].astype(F32), blank], 0).astype(BF)
    for out, row in zip((far, near), near_and_far(faces[1:2], faces[0:1])):
        out[:sites] = grad
        picks = face_sites(row, sites).T.astype(BF)
        out[sites : sites + rim] = dot(picks, masked).astype(BF)
        out[sites + rim :] = names


def stage_kernel(
    counts, feat, own, sides, w_one_in, w_two_in,
    masked, grad, names, faces, picks, w_one, w_two, sems,
):
    sites, rim = feat.shape[0], sides.shape[1]
    live = live_rows(counts, sites)
    masked[...] = jnp.where(live, feat[...].astype(F32), 0.0).astype(BF)
    grad[...] = own[:sites]
    names[...] = own[sites + rim :].astype(F32)
    faces[...] = sides[...]
    columns = names[...].T
    for k in range(picks.shape[0]):
        picks[k] = pick_matrix(columns, k)
        w_one[k] = w_one_in[k]
        w_two[k] = w_two_in[k]


def sites_of(names, first, row):
    found = jnp.full(names.shape, NOWHERE, F32)
    for j in range(row.shape[1]):
        found = jnp.where(names == first + j, row[:, j : j + 1], found)
    return found


def lanes(k, width, n=1):
    return slice(k * width, (k + n) * width)


def back(held, w_ref, rows):
    offsets, channels = w_ref.shape[0], w_ref.shape[1]
    total = jnp.zeros((rows, channels), F32)
    for k in range(0, offsets, 2):
        n = min(2, offsets - k)
        weight = jnp.concatenate([w_ref[k + j] for j in range(n)], 1)
        total = total + dot(held[:, lanes(k, w_ref.shape[2], n)], weight, (1, 1))
    return total


def main_kernel(
    counts, masked, own_grads, own_names, faces, picks, w_one, w_two, far, near,
    far_out, own_grad, hidden_ref, mine, theirs,
    picked, held, kept, sems,
):
    offsets, channels = w_one.shape[0], w_one.shape[1]
    sites, rim = masked.shape[0], faces.shape[1]
    live = live_rows(counts, sites)
    above = near_is_above()
    near_row, far_row = near_and_far(faces[0:1], faces[1:2])
    rims = slice(sites, sites + rim)
    near_rim, far_rim = near[rims].astype(F32), far[rims].astype(F32)
    extended = extend(
        masked[...].astype(F32),
        jnp.where(above, far_rim, near_rim),
        jnp.where(above, near_rim, far_rim),
    )
    for k in range(offsets):
        picked[:, lanes(k, channels)] = dot(picks[k], extended).astype(BF)
    x = dot(picked[...], w_one[...].reshape(offsets * channels, channels))

    up_first, down_first = float(sites), float(sites + rim)
    near_first = jnp.where(above, up_first, down_first)
    far_first = jnp.where(above, down_first, up_first)
    names = jnp.concatenate(
        [
            own_names[...],
            sites_of(near[sites + rim :].astype(F32), near_first, near_row),
            sites_of(far[sites + rim :].astype(F32), far_first, far_row),
        ],
        1,
    )
    grads = jnp.concatenate([own_grads[...], near[:sites], far[:sites]], 0)
    rows = iota((sites, 3 * sites), 0)
    for k in range(offsets):
        hits = jnp.where(rows == names[k : k + 1], 1.0, 0.0).astype(BF)
        held[:, lanes(k, channels)] = dot(hits, grads).astype(BF)
    hidden_grad = back(held, w_two, sites)

    slope = math.sqrt(2.0 / math.pi)
    t = jnp.tanh(slope * (x + 0.044715 * (x * x * x)))
    cdf = 0.5 * (1.0 + t)
    hidden = jnp.where(live, x * cdf, 0.0)
    hidden_ref[...] = hidden.astype(BF)
    bend = cdf + 0.5 * x * (1.0 - t * t) * (slope * (1.0 + 3 * 0.044715 * (x * x)))
    pre_grad = jnp.where(live, bend * hidden_grad, 0.0).astype(BF)

    extended_t = extended.astype(F32).T.astype(BF)
    hidden_t = hidden.T.astype(BF)
    rows = iota((WIDE, sites), 0)
    for k in range(offsets):
        hits = jnp.where(rows == names[k : k + 1, :sites], 1.0, 0.0).astype(BF)
        kept[:, lanes(k, channels)] = dot(hits, pre_grad).astype(BF)
    ext_grad = back(kept, w_one, WIDE)
    own_grad[...] = ext_grad[:sites]
    to_above, to_below = ext_grad[sites + rim : sites + 2 * rim], ext_grad[rims]
    near_pick = face_sites(near_row, sites).T.astype(BF)
    far_pick = face_sites(far_row, sites).T.astype(BF)
    to_near = jnp.where(above, to_above, to_below)
    coarse = to_near.astype(BF)
    theirs[offsets, :rim] = dot(near_pick, hidden.astype(BF)).astype(BF)
    theirs[offsets, rim : 2 * rim] = coarse
    theirs[offsets, 2 * rim : 3 * rim] = (to_near - coarse.astype(F32)).astype(BF)
    theirs[offsets, 3 * rim :] = jnp.zeros((channels - 3 * rim, channels), BF)
    far_out[:rim] = dot(far_pick, hidden.astype(BF))
    far_out[rim:] = jnp.where(above, to_below, to_above)
    first_is_mine = lax.axis_index("core") == 0
    for k in range(0, offsets, 2):
        n = min(2, offsets - k)
        first = dot(extended_t, kept[:, lanes(k, channels, n)])
        second = dot(hidden_t, held[:, lanes(k, channels, n)])
        for j in range(n):
            a, b = first[:, lanes(j, channels)], second[:, lanes(j, channels)]
            mine[k + j] = jnp.where(first_is_mine, a, b).astype(BF)
            theirs[k + j] = jnp.where(first_is_mine, b, a).astype(BF)
    mine[offsets] = jnp.zeros((channels, channels), BF)


def last_kernel(
    counts, hidden, faces, near, far, own_grad, picks, w_two,
    response, input_grad, picked, sems,
):
    sites, rim = hidden.shape[0], faces.shape[1]
    offsets, channels = w_two.shape[0], w_two.shape[1]
    live = live_rows(counts, sites)
    above = near_is_above()
    near_row, far_row = near_and_far(faces[0:1], faces[1:2])
    near_grad = near[rim : 2 * rim].astype(F32) + near[2 * rim : 3 * rim].astype(F32)
    grad = own_grad[...] + dot(face_sites(near_row, sites), near_grad, exact=True)
    grad = grad + dot(face_sites(far_row, sites), far[rim:], exact=True)
    input_grad[...] = jnp.where(live, grad, 0.0).astype(BF)
    near_rim = near[:rim].astype(F32)
    extended = extend(
        hidden[...].astype(F32),
        jnp.where(above, far[:rim], near_rim),
        jnp.where(above, near_rim, far[:rim]),
    )
    for k in range(offsets):
        picked[:, lanes(k, channels)] = dot(picks[k], extended).astype(BF)
    second_pre = dot(picked[...], w_two[...].reshape(offsets * channels, channels))
    response[...] = jnp.where(live, second_pre, 0.0).astype(BF)


def call(kernel, places, outs, scratch, copies, us, limit=16):
    spec = {
        "s": pl.BlockSpec(memory_space=pltpu.SMEM),
        "v": pl.BlockSpec(memory_space=pltpu.VMEM),
        "h": pl.BlockSpec(memory_space=pltpu.HBM),
    }
    return pl.pallas_call(
        kernel,
        out_shape=[jax.ShapeDtypeStruct(s, d) for s, d in outs],
        in_specs=[spec[p] for p in places],
        out_specs=[pl.BlockSpec(memory_space=pltpu.VMEM)] * len(outs),
        scratch_shapes=[pltpu.VMEM(s, d) for s, d in scratch]
        + [pltpu.SemaphoreType.DMA((copies,))],
        compiler_params=pltpu.CompilerParams(vmem_limit_bytes=limit * 2**20),
        cost_estimate=pl.CostEstimate(
            flops=0, bytes_accessed=int(us * 3e6), transcendentals=0
        ),
    )


def far_slab(block):
    last = lax.axis_size(SLAB) - 1
    pairs = [p for i in range(1, last, 2) for p in ((i, i + 1), (i + 1, i))]
    return lax.ppermute(block, SLAB, pairs)


def swap(block, axis):
    return lax.all_to_all(block, axis, 0, 0, tiled=True)


def other_core(block):
    return lax.ppermute(block, "core", [(0, 1), (1, 0)])


def on_device(feat, counts, nb, low, high, w_one, w_two, cot):
    sites, channels = feat.shape
    offsets, rim = nb.shape[1], low.shape[0]
    scaling = 1.0 / math.sqrt(lax.axis_size(AXES) * sites)
    half = math.sqrt(scaling)
    flat = ((sites, channels), BF)
    field = ((sites, channels), F32)
    message = ((sites + 2 * rim, channels), BF)
    ends = ((2 * rim, channels), F32)
    weight = ((offsets, channels, channels), BF)
    sums = ((offsets + 1, channels, channels), BF)
    row = ((1, rim), jnp.int32)
    faces = ((2, rim), F32)
    picks = ((offsets, sites, WIDE), BF)
    broad = ((sites, offsets * channels), BF)
    low, high, table = low.reshape(1, rim), high.reshape(1, rim), nb.T
    letters = call(
        pack_kernel, "shhhhh", (message, message, faces),
        (flat, flat, ((offsets, sites), jnp.int32), row, row), 5, 1, limit=60,
    )(counts, feat, cot, table, low, high)
    masked, grad, names, faces, picks, w_one, w_two = call(
        stage_kernel, "svvvvv",
        (flat, flat, ((rim, sites), F32), faces, picks, weight, weight), (), 1, 2,
    )(counts, feat, letters[1], letters[2], w_one, w_two)
    near, far = other_core(letters[0]), far_slab(letters[1])
    far_two, own_grad, hidden, mine, theirs = call(
        main_kernel, "svvvvvvvvv", (ends, field, flat, sums, sums),
        (broad, broad, ((WIDE, offsets * channels), BF)), 1, 5,
    )(counts, masked, grad, names, faces, picks, w_one, w_two, far, near)

    column, block = lax.axis_size(COLUMN), lax.axis_size(BLOCK)
    near = other_core(theirs)
    far = far_slab(far_two)
    share = (mine.astype(F32) + near.astype(F32)).astype(BF)
    far, share = lax.optimization_barrier((far, share))
    parts = swap(share.reshape(block, -1, channels), BLOCK)
    parts = (jnp.sum(parts.astype(F32), 0) * half).astype(BF)
    parts = swap(jnp.broadcast_to(parts, (column, *parts.shape)), COLUMN)
    response, input_grad = call(
        last_kernel, "svvvvvvv", (flat, flat), (broad,), 1, 3
    )(counts, hidden, faces, near[offsets], far, own_grad, picks, w_two)
    total = (jnp.sum(parts.astype(F32), 0) * half).astype(BF)
    total, response, input_grad = lax.optimization_barrier((total, response, input_grad))

    whole = swap(jnp.broadcast_to(total, (block, *total.shape)), BLOCK)
    whole = whole.reshape(offsets + 1, channels, channels)
    other = other_core(whole)
    first_is_mine = lax.axis_index("core") == 0
    first = jnp.where(first_is_mine, whole, other)[:offsets]
    second = jnp.where(first_is_mine, other, whole)[:offsets]
    return response, input_grad, first, second


def solution(mesh):
    groups, slabs = mesh.devices.shape
    side = {64: 4, 16: 2, 4: 1}[slabs]
    pair = 2 if groups % 2 == 0 else 1
    fine = Mesh(mesh.devices.reshape(groups // pair, pair, side, side, 2, 2), AXES)
    rows, row = P(AXES, None), P(AXES)
    return jax.shard_map(
        on_device,
        mesh=fine,
        in_specs=(rows, row, rows, row, row, P(), P(), rows),
        out_specs=(rows, rows, P(), P()),
        check_vma=False,
    )
```

```python
import math

import jax
import jax.numpy as jnp
from jax import lax
from jax.experimental import pallas as pl
from jax.experimental.pallas import tpu as pltpu
from jax.sharding import Mesh, PartitionSpec as P

AXES = ("column", "pair", "y", "x", "zh", "core")
SLAB = ("y", "x", "zh", "core")
PLANE = ("y", "x")
COLUMN = ("column", "zh")
BF = jnp.bfloat16
F32 = jnp.float32
WIDE = 256
NOWHERE = 255.0


def dot(a, b, contract=(1, 0), exact=False):
    return lax.dot_general(
        a,
        b,
        (((contract[0],), (contract[1],)), ((), ())),
        preferred_element_type=F32,
        precision=lax.Precision.HIGHEST if exact else None,
    )


def iota(shape, dim):
    return lax.broadcasted_iota(jnp.int32, shape, dim).astype(F32)


def live_rows(counts_ref, sites):
    return lax.broadcasted_iota(jnp.int32, (sites, 1), 0) < counts_ref[0]


def face_sites(row, sites):
    return (iota((sites, row.shape[1]), 0) == row).astype(F32)


def pick_matrix(columns, k):
    sites = columns.shape[0]
    return jnp.where(iota((sites, WIDE), 1) == columns[:, k : k + 1], 1.0, 0.0).astype(BF)


def gather_conv(extended, picks, w_ref):
    total = jnp.zeros((w_ref.shape[1], w_ref.shape[2]), F32)
    for k in range(w_ref.shape[0]):
        total = total + dot(dot(picks(k), extended).astype(BF), w_ref[k])
    return total


def extend(values, below, above):
    rim = below.shape[0]
    pad = jnp.zeros((WIDE - values.shape[0] - 2 * rim, values.shape[1]), F32)
    return jnp.concatenate([values, below, above, pad], 0).astype(BF)


def fetch(sources, targets, sems):
    copies = [
        pltpu.make_async_copy(s, t, sems.at[i])
        for i, (s, t) in enumerate(zip(sources, targets))
    ]
    for copy in copies:
        copy.start()
    return copies


def near_is_above():
    return lax.axis_index("core") == 0


def near_and_far(low, high):
    above = near_is_above()
    return jnp.where(above, high, low), jnp.where(above, low, high)


def pack_kernel(
    counts, feat_h, cot_h, map_h, low_h, high_h, near, far, faces,
    feat, cot, table, low, high, sems,
):
    for copy in fetch(
        (feat_h, cot_h, map_h, low_h, high_h), (feat, cot, table, low, high), sems
    ):
        copy.wait()
    live = live_rows(counts, feat.shape[0])
    faces[0:1] = low[...].astype(F32)
    faces[1:2] = high[...].astype(F32)
    offsets, sites = table.shape
    rim = low.shape[1]
    masked = jnp.where(live, feat[...].astype(F32), 0.0).astype(BF)
    grad = jnp.where(live, cot[...].astype(F32), 0.0).astype(BF)
    blank = jnp.full((rim - offsets, sites), NOWHERE, F32)
    names = jnp.concatenate([table[...].astype(F32), blank], 0).astype(BF)
    for out, row in zip((far, near), near_and_far(faces[1:2], faces[0:1])):
        out[:sites] = grad
        picks = face_sites(row, sites).T.astype(BF)
        out[sites : sites + rim] = dot(picks, masked).astype(BF)
        out[sites + rim :] = names


def stage_kernel(
    counts, feat, own, sides, w_one_in, w_two_in,
    masked, grad, names, faces, picks, w_one, w_two, sems,
):
    sites, rim = feat.shape[0], sides.shape[1]
    live = live_rows(counts, sites)
    masked[...] = jnp.where(live, feat[...].astype(F32), 0.0).astype(BF)
    grad[...] = own[:sites]
    names[...] = own[sites + rim :].astype(F32)
    faces[...] = sides[...]
    columns = names[...].T
    for k in range(picks.shape[0]):
        picks[k] = pick_matrix(columns, k)
        w_one[k] = w_one_in[k]
        w_two[k] = w_two_in[k]


def sites_of(names, first, row):
    found = jnp.full(names.shape, NOWHERE, F32)
    for j in range(row.shape[1]):
        found = jnp.where(names == first + j, row[:, j : j + 1], found)
    return found


def lanes(k, width, n=1):
    return slice(k * width, (k + n) * width)


def back(held, w_ref, rows):
    offsets, channels = w_ref.shape[0], w_ref.shape[1]
    total = jnp.zeros((rows, channels), F32)
    for k in range(0, offsets, 2):
        n = min(2, offsets - k)
        weight = jnp.concatenate([w_ref[k + j] for j in range(n)], 1)
        total = total + dot(held[:, lanes(k, w_ref.shape[2], n)], weight, (1, 1))
    return total


def main_kernel(
    counts, masked, own_grads, own_names, faces, picks, w_one, w_two, far, near,
    far_out, own_grad, hidden_ref, mine, theirs,
    picked, held, kept, sems,
):
    offsets, channels = w_one.shape[0], w_one.shape[1]
    sites, rim = masked.shape[0], faces.shape[1]
    live = live_rows(counts, sites)
    above = near_is_above()
    near_row, far_row = near_and_far(faces[0:1], faces[1:2])
    rims = slice(sites, sites + rim)
    near_rim, far_rim = near[rims].astype(F32), far[rims].astype(F32)
    extended = extend(
        masked[...].astype(F32),
        jnp.where(above, far_rim, near_rim),
        jnp.where(above, near_rim, far_rim),
    )
    for k in range(offsets):
        picked[:, lanes(k, channels)] = dot(picks[k], extended).astype(BF)
    x = dot(picked[...], w_one[...].reshape(offsets * channels, channels))

    up_first, down_first = float(sites), float(sites + rim)
    near_first = jnp.where(above, up_first, down_first)
    far_first = jnp.where(above, down_first, up_first)
    names = jnp.concatenate(
        [
            own_names[...],
            sites_of(near[sites + rim :].astype(F32), near_first, near_row),
            sites_of(far[sites + rim :].astype(F32), far_first, far_row),
        ],
        1,
    )
    grads = jnp.concatenate([own_grads[...], near[:sites], far[:sites]], 0)
    rows = iota((sites, 3 * sites), 0)
    for k in range(offsets):
        hits = jnp.where(rows == names[k : k + 1], 1.0, 0.0).astype(BF)
        held[:, lanes(k, channels)] = dot(hits, grads).astype(BF)
    hidden_grad = back(held, w_two, sites)

    slope = math.sqrt(2.0 / math.pi)
    t = jnp.tanh(slope * (x + 0.044715 * (x * x * x)))
    cdf = 0.5 * (1.0 + t)
    hidden = jnp.where(live, x * cdf, 0.0)
    hidden_ref[...] = hidden.astype(BF)
    bend = cdf + 0.5 * x * (1.0 - t * t) * (slope * (1.0 + 3 * 0.044715 * (x * x)))
    pre_grad = jnp.where(live, bend * hidden_grad, 0.0).astype(BF)

    extended_t = extended.astype(F32).T.astype(BF)
    hidden_t = hidden.T.astype(BF)
    rows = iota((WIDE, sites), 0)
    for k in range(offsets):
        hits = jnp.where(rows == names[k : k + 1, :sites], 1.0, 0.0).astype(BF)
        kept[:, lanes(k, channels)] = dot(hits, pre_grad).astype(BF)
    ext_grad = back(kept, w_one, WIDE)
    own_grad[...] = ext_grad[:sites]
    to_above, to_below = ext_grad[sites + rim : sites + 2 * rim], ext_grad[rims]
    near_pick = face_sites(near_row, sites).T.astype(BF)
    far_pick = face_sites(far_row, sites).T.astype(BF)
    to_near = jnp.where(above, to_above, to_below)
    coarse = to_near.astype(BF)
    theirs[offsets, :rim] = dot(near_pick, hidden.astype(BF)).astype(BF)
    theirs[offsets, rim : 2 * rim] = coarse
    theirs[offsets, 2 * rim : 3 * rim] = (to_near - coarse.astype(F32)).astype(BF)
    theirs[offsets, 3 * rim :] = jnp.zeros((channels - 3 * rim, channels), BF)
    far_out[:rim] = dot(far_pick, hidden.astype(BF))
    far_out[rim:] = jnp.where(above, to_below, to_above)
    first_is_mine = lax.axis_index("core") == 0
    for k in range(0, offsets, 2):
        n = min(2, offsets - k)
        first = dot(extended_t, kept[:, lanes(k, channels, n)])
        second = dot(hidden_t, held[:, lanes(k, channels, n)])
        for j in range(n):
            a, b = first[:, lanes(j, channels)], second[:, lanes(j, channels)]
            mine[k + j] = jnp.where(first_is_mine, a, b).astype(BF)
            theirs[k + j] = jnp.where(first_is_mine, b, a).astype(BF)
    mine[offsets] = jnp.zeros((channels, channels), BF)


def last_kernel(
    counts, hidden, faces, near, far, own_grad, picks, w_two,
    response, input_grad, picked, sems,
):
    sites, rim = hidden.shape[0], faces.shape[1]
    offsets, channels = w_two.shape[0], w_two.shape[1]
    live = live_rows(counts, sites)
    above = near_is_above()
    near_row, far_row = near_and_far(faces[0:1], faces[1:2])
    near_grad = near[rim : 2 * rim].astype(F32) + near[2 * rim : 3 * rim].astype(F32)
    grad = own_grad[...] + dot(face_sites(near_row, sites), near_grad, exact=True)
    grad = grad + dot(face_sites(far_row, sites), far[rim:], exact=True)
    input_grad[...] = jnp.where(live, grad, 0.0).astype(BF)
    near_rim = near[:rim].astype(F32)
    extended = extend(
        hidden[...].astype(F32),
        jnp.where(above, far[:rim], near_rim),
        jnp.where(above, near_rim, far[:rim]),
    )
    for k in range(offsets):
        picked[:, lanes(k, channels)] = dot(picks[k], extended).astype(BF)
    second_pre = dot(picked[...], w_two[...].reshape(offsets * channels, channels))
    response[...] = jnp.where(live, second_pre, 0.0).astype(BF)


def call(kernel, places, outs, scratch, copies, us, limit=16):
    spec = {
        "s": pl.BlockSpec(memory_space=pltpu.SMEM),
        "v": pl.BlockSpec(memory_space=pltpu.VMEM),
        "h": pl.BlockSpec(memory_space=pltpu.HBM),
    }
    return pl.pallas_call(
        kernel,
        out_shape=[jax.ShapeDtypeStruct(s, d) for s, d in outs],
        in_specs=[spec[p] for p in places],
        out_specs=[pl.BlockSpec(memory_space=pltpu.VMEM)] * len(outs),
        scratch_shapes=[pltpu.VMEM(s, d) for s, d in scratch]
        + [pltpu.SemaphoreType.DMA((copies,))],
        compiler_params=pltpu.CompilerParams(vmem_limit_bytes=limit * 2**20),
        cost_estimate=pl.CostEstimate(
            flops=0, bytes_accessed=int(us * 3e6), transcendentals=0
        ),
    )


def far_slab(block):
    last = lax.axis_size(SLAB) - 1
    pairs = [p for i in range(1, last, 2) for p in ((i, i + 1), (i + 1, i))]
    return lax.ppermute(block, SLAB, pairs)


def swap(block, axis):
    return lax.all_to_all(block, axis, 0, 0, tiled=True)


def other_core(block):
    return lax.ppermute(block, "core", [(0, 1), (1, 0)])


def other_plane(block):
    return lax.ppermute(block, "pair", [(0, 1), (1, 0)])


def on_device(feat, counts, nb, low, high, w_one, w_two, cot):
    sites, channels = feat.shape
    offsets, rim = nb.shape[1], low.shape[0]
    scaling = 1.0 / math.sqrt(lax.axis_size(AXES) * sites)
    half = math.sqrt(scaling)
    flat = ((sites, channels), BF)
    field = ((sites, channels), F32)
    message = ((sites + 2 * rim, channels), BF)
    ends = ((2 * rim, channels), F32)
    weight = ((offsets, channels, channels), BF)
    sums = ((offsets + 1, channels, channels), BF)
    row = ((1, rim), jnp.int32)
    faces = ((2, rim), F32)
    picks = ((offsets, sites, WIDE), BF)
    broad = ((sites, offsets * channels), BF)
    low, high, table = low.reshape(1, rim), high.reshape(1, rim), nb.T
    letters = call(
        pack_kernel, "shhhhh", (message, message, faces),
        (flat, flat, ((offsets, sites), jnp.int32), row, row), 5, 1, limit=60,
    )(counts, feat, cot, table, low, high)
    masked, grad, names, faces, picks, w_one, w_two = call(
        stage_kernel, "svvvvv",
        (flat, flat, ((rim, sites), F32), faces, picks, weight, weight), (), 1, 2,
    )(counts, feat, letters[1], letters[2], w_one, w_two)
    near, far = other_core(letters[0]), far_slab(letters[1])
    far_two, own_grad, hidden, mine, theirs = call(
        main_kernel, "svvvvvvvvv", (ends, field, flat, sums, sums),
        (broad, broad, ((WIDE, offsets * channels), BF)), 1, 5,
    )(counts, masked, grad, names, faces, picks, w_one, w_two, far, near)

    column, plane = lax.axis_size(COLUMN), lax.axis_size(PLANE)
    side = lax.axis_index("pair")
    near = other_core(theirs)
    share = (mine.astype(F32) + near.astype(F32)).astype(BF)
    share, far_two = lax.optimization_barrier((share, far_two))
    parts = swap(share.reshape(plane, -1, channels), PLANE)
    far = far_slab(far_two)
    parts = jnp.sum(parts.astype(F32), 0)
    parts, far = lax.optimization_barrier((parts, far))
    rows = parts.shape[0] // 2
    keep = lax.dynamic_slice_in_dim(parts, side * rows, rows)
    give = lax.dynamic_slice_in_dim(parts, (1 - side) * rows, rows)
    parts = ((keep + other_plane(give)) * half).astype(BF)
    parts = swap(jnp.broadcast_to(parts, (column, *parts.shape)), COLUMN)
    response, input_grad = call(
        last_kernel, "svvvvvvv", (flat, flat), (broad,), 1, 3
    )(counts, hidden, faces, near[offsets], far, own_grad, picks, w_two)
    total = (jnp.sum(parts.astype(F32), 0) * half).astype(BF)
    total, response, input_grad = lax.optimization_barrier((total, response, input_grad))

    other = other_plane(total)
    both = jnp.where(
        side == 0, jnp.concatenate([total, other]), jnp.concatenate([other, total])
    )
    whole = swap(jnp.broadcast_to(both, (plane, *both.shape)), PLANE)
    whole = whole.reshape(offsets + 1, channels, channels)
    other = other_core(whole)
    first_is_mine = lax.axis_index("core") == 0
    first = jnp.where(first_is_mine, whole, other)[:offsets]
    second = jnp.where(first_is_mine, other, whole)[:offsets]
    return response, input_grad, first, second


def solution(mesh):
    groups, slabs = mesh.devices.shape
    side = {64: 4, 16: 2, 4: 1}[slabs]
    pair = 2 if groups % 2 == 0 else 1
    fine = Mesh(mesh.devices.reshape(groups // pair, pair, side, side, 2, 2), AXES)
    rows, row = P(AXES, None), P(AXES)
    return jax.shard_map(
        on_device,
        mesh=fine,
        in_specs=(rows, row, rows, row, row, P(), P(), rows),
        out_specs=(rows, rows, P(), P()),
        check_vma=False,
    )
```

```python
import math

import jax
import jax.numpy as jnp
from jax import lax
from jax.experimental import pallas as pl
from jax.experimental.pallas import tpu as pltpu
from jax.sharding import Mesh, PartitionSpec as P

AXES = ("column", "pair", "y", "x", "zh", "core")
SLAB = ("y", "x", "zh", "core")
BLOCK = ("y", "x", "pair")
COLUMN = ("column", "zh")
BF = jnp.bfloat16
F32 = jnp.float32
WIDE = 256
NOWHERE = 255.0


def dot(a, b, contract=(1, 0), exact=False):
    return lax.dot_general(
        a,
        b,
        (((contract[0],), (contract[1],)), ((), ())),
        preferred_element_type=F32,
        precision=lax.Precision.HIGHEST if exact else None,
    )


def iota(shape, dim):
    return lax.broadcasted_iota(jnp.int32, shape, dim).astype(F32)


def live_rows(counts_ref, sites):
    return lax.broadcasted_iota(jnp.int32, (sites, 1), 0) < counts_ref[0]


def face_sites(row, sites):
    return (iota((sites, row.shape[1]), 0) == row).astype(F32)


def pick_matrix(columns, k):
    sites = columns.shape[0]
    return jnp.where(iota((sites, WIDE), 1) == columns[:, k : k + 1], 1.0, 0.0).astype(BF)


def gather_conv(extended, picks, w_ref):
    total = jnp.zeros((w_ref.shape[1], w_ref.shape[2]), F32)
    for k in range(w_ref.shape[0]):
        total = total + dot(dot(picks(k), extended).astype(BF), w_ref[k])
    return total


def extend(values, below, above):
    rim = below.shape[0]
    pad = jnp.zeros((WIDE - values.shape[0] - 2 * rim, values.shape[1]), F32)
    return jnp.concatenate([values, below, above, pad], 0).astype(BF)


def fetch(sources, targets, sems):
    copies = [
        pltpu.make_async_copy(s, t, sems.at[i])
        for i, (s, t) in enumerate(zip(sources, targets))
    ]
    for copy in copies:
        copy.start()
    return copies


def near_is_above():
    return lax.axis_index("core") == 0


def near_and_far(low, high):
    above = near_is_above()
    return jnp.where(above, high, low), jnp.where(above, low, high)


def pack_kernel(
    counts, feat_h, cot_h, map_h, low_h, high_h, near, far, faces,
    feat, cot, table, low, high, sems,
):
    for copy in fetch(
        (feat_h, cot_h, map_h, low_h, high_h), (feat, cot, table, low, high), sems
    ):
        copy.wait()
    live = live_rows(counts, feat.shape[0])
    faces[0:1] = low[...].astype(F32)
    faces[1:2] = high[...].astype(F32)
    offsets, sites = table.shape
    rim = low.shape[1]
    masked = jnp.where(live, feat[...].astype(F32), 0.0).astype(BF)
    grad = jnp.where(live, cot[...].astype(F32), 0.0).astype(BF)
    blank = jnp.full((rim - offsets, sites), NOWHERE, F32)
    names = jnp.concatenate([table[...].astype(F32), blank], 0).astype(BF)
    for out, row in zip((far, near), near_and_far(faces[1:2], faces[0:1])):
        out[:sites] = grad
        picks = face_sites(row, sites).T.astype(BF)
        out[sites : sites + rim] = dot(picks, masked).astype(BF)
        out[sites + rim :] = names


def stage_kernel(
    counts, feat, own, sides, w_one_in, w_two_in,
    masked, grad, names, faces, picks, w_one, w_two, sems,
):
    sites, rim = feat.shape[0], sides.shape[1]
    live = live_rows(counts, sites)
    masked[...] = jnp.where(live, feat[...].astype(F32), 0.0).astype(BF)
    grad[...] = own[:sites]
    names[...] = own[sites + rim :].astype(F32)
    faces[...] = sides[...]
    columns = names[...].T
    for k in range(picks.shape[0]):
        picks[k] = pick_matrix(columns, k)
        w_one[k] = w_one_in[k]
        w_two[k] = w_two_in[k]


def sites_of(names, first, row):
    found = jnp.full(names.shape, NOWHERE, F32)
    for j in range(row.shape[1]):
        found = jnp.where(names == first + j, row[:, j : j + 1], found)
    return found


def lanes(k, width, n=1):
    return slice(k * width, (k + n) * width)


def back(held, w_ref, rows):
    offsets, channels = w_ref.shape[0], w_ref.shape[1]
    total = jnp.zeros((rows, channels), F32)
    for k in range(0, offsets, 2):
        n = min(2, offsets - k)
        weight = jnp.concatenate([w_ref[k + j] for j in range(n)], 1)
        total = total + dot(held[:, lanes(k, w_ref.shape[2], n)], weight, (1, 1))
    return total


def main_kernel(
    counts, masked, own_grads, own_names, faces, picks, w_one, w_two, far, near,
    far_out, own_grad, hidden_ref, mine, theirs,
    picked, held, kept, sems,
):
    offsets, channels = w_one.shape[0], w_one.shape[1]
    sites, rim = masked.shape[0], faces.shape[1]
    live = live_rows(counts, sites)
    above = near_is_above()
    near_row, far_row = near_and_far(faces[0:1], faces[1:2])
    rims = slice(sites, sites + rim)
    near_rim, far_rim = near[rims].astype(F32), far[rims].astype(F32)
    extended = extend(
        masked[...].astype(F32),
        jnp.where(above, far_rim, near_rim),
        jnp.where(above, near_rim, far_rim),
    )
    for k in range(offsets):
        picked[:, lanes(k, channels)] = dot(picks[k], extended).astype(BF)
    x = dot(picked[...], w_one[...].reshape(offsets * channels, channels))

    up_first, down_first = float(sites), float(sites + rim)
    near_first = jnp.where(above, up_first, down_first)
    far_first = jnp.where(above, down_first, up_first)
    names = jnp.concatenate(
        [
            own_names[...],
            sites_of(near[sites + rim :].astype(F32), near_first, near_row),
            sites_of(far[sites + rim :].astype(F32), far_first, far_row),
        ],
        1,
    )
    grads = jnp.concatenate([own_grads[...], near[:sites], far[:sites]], 0)
    rows = iota((sites, 3 * sites), 0)
    for k in range(offsets):
        hits = jnp.where(rows == names[k : k + 1], 1.0, 0.0).astype(BF)
        held[:, lanes(k, channels)] = dot(hits, grads).astype(BF)
    hidden_grad = back(held, w_two, sites)

    slope = math.sqrt(2.0 / math.pi)
    t = jnp.tanh(slope * (x + 0.044715 * (x * x * x)))
    cdf = 0.5 * (1.0 + t)
    hidden = jnp.where(live, x * cdf, 0.0)
    hidden_ref[...] = hidden.astype(BF)
    bend = cdf + 0.5 * x * (1.0 - t * t) * (slope * (1.0 + 3 * 0.044715 * (x * x)))
    pre_grad = jnp.where(live, bend * hidden_grad, 0.0).astype(BF)

    extended_t = extended.astype(F32).T.astype(BF)
    hidden_t = hidden.T.astype(BF)
    rows = iota((WIDE, sites), 0)
    for k in range(offsets):
        hits = jnp.where(rows == names[k : k + 1, :sites], 1.0, 0.0).astype(BF)
        kept[:, lanes(k, channels)] = dot(hits, pre_grad).astype(BF)
    ext_grad = back(kept, w_one, WIDE)
    own_grad[...] = ext_grad[:sites]
    to_above, to_below = ext_grad[sites + rim : sites + 2 * rim], ext_grad[rims]
    near_pick = face_sites(near_row, sites).T.astype(BF)
    far_pick = face_sites(far_row, sites).T.astype(BF)
    to_near = jnp.where(above, to_above, to_below)
    coarse = to_near.astype(BF)
    theirs[offsets, :rim] = dot(near_pick, hidden.astype(BF)).astype(BF)
    theirs[offsets, rim : 2 * rim] = coarse
    theirs[offsets, 2 * rim : 3 * rim] = (to_near - coarse.astype(F32)).astype(BF)
    theirs[offsets, 3 * rim :] = jnp.zeros((channels - 3 * rim, channels), BF)
    far_out[:rim] = dot(far_pick, hidden.astype(BF))
    far_out[rim:] = jnp.where(above, to_below, to_above)
    first_is_mine = lax.axis_index("core") == 0
    for k in range(0, offsets, 2):
        n = min(2, offsets - k)
        first = dot(extended_t, kept[:, lanes(k, channels, n)])
        second = dot(hidden_t, held[:, lanes(k, channels, n)])
        for j in range(n):
            a, b = first[:, lanes(j, channels)], second[:, lanes(j, channels)]
            mine[k + j] = jnp.where(first_is_mine, a, b).astype(BF)
            theirs[k + j] = jnp.where(first_is_mine, b, a).astype(BF)
    mine[offsets] = jnp.zeros((channels, channels), BF)


def last_kernel(
    counts, hidden, faces, near, far, own_grad, picks, w_two,
    response, input_grad, picked, sems,
):
    sites, rim = hidden.shape[0], faces.shape[1]
    offsets, channels = w_two.shape[0], w_two.shape[1]
    live = live_rows(counts, sites)
    above = near_is_above()
    near_row, far_row = near_and_far(faces[0:1], faces[1:2])
    near_grad = near[rim : 2 * rim].astype(F32) + near[2 * rim : 3 * rim].astype(F32)
    grad = own_grad[...] + dot(face_sites(near_row, sites), near_grad, exact=True)
    grad = grad + dot(face_sites(far_row, sites), far[rim:], exact=True)
    input_grad[...] = jnp.where(live, grad, 0.0).astype(BF)
    near_rim = near[:rim].astype(F32)
    extended = extend(
        hidden[...].astype(F32),
        jnp.where(above, far[:rim], near_rim),
        jnp.where(above, near_rim, far[:rim]),
    )
    for k in range(offsets):
        picked[:, lanes(k, channels)] = dot(picks[k], extended).astype(BF)
    second_pre = dot(picked[...], w_two[...].reshape(offsets * channels, channels))
    response[...] = jnp.where(live, second_pre, 0.0).astype(BF)


def call(kernel, places, outs, scratch, copies, us, limit=16):
    spec = {
        "s": pl.BlockSpec(memory_space=pltpu.SMEM),
        "v": pl.BlockSpec(memory_space=pltpu.VMEM),
        "h": pl.BlockSpec(memory_space=pltpu.HBM),
    }
    return pl.pallas_call(
        kernel,
        out_shape=[jax.ShapeDtypeStruct(s, d) for s, d in outs],
        in_specs=[spec[p] for p in places],
        out_specs=[pl.BlockSpec(memory_space=pltpu.VMEM)] * len(outs),
        scratch_shapes=[pltpu.VMEM(s, d) for s, d in scratch]
        + [pltpu.SemaphoreType.DMA((copies,))],
        compiler_params=pltpu.CompilerParams(vmem_limit_bytes=limit * 2**20),
        cost_estimate=pl.CostEstimate(
            flops=0, bytes_accessed=int(us * 3e6), transcendentals=0
        ),
    )


def far_slab(block):
    last = lax.axis_size(SLAB) - 1
    pairs = [p for i in range(1, last, 2) for p in ((i, i + 1), (i + 1, i))]
    return lax.ppermute(block, SLAB, pairs)


def swap(block, axis):
    return lax.all_to_all(block, axis, 0, 0, tiled=True)


def other_core(block):
    return lax.ppermute(block, "core", [(0, 1), (1, 0)])


def on_device(feat, counts, nb, low, high, w_one, w_two, cot):
    sites, channels = feat.shape
    offsets, rim = nb.shape[1], low.shape[0]
    scaling = 1.0 / math.sqrt(lax.axis_size(AXES) * sites)
    half = math.sqrt(scaling)
    flat = ((sites, channels), BF)
    field = ((sites, channels), F32)
    message = ((sites + 2 * rim, channels), BF)
    ends = ((2 * rim, channels), F32)
    weight = ((offsets, channels, channels), BF)
    sums = ((offsets + 1, channels, channels), BF)
    row = ((1, rim), jnp.int32)
    faces = ((2, rim), F32)
    picks = ((offsets, sites, WIDE), BF)
    broad = ((sites, offsets * channels), BF)
    low, high, table = low.reshape(1, rim), high.reshape(1, rim), nb.T
    letters = call(
        pack_kernel, "shhhhh", (message, message, faces),
        (flat, flat, ((offsets, sites), jnp.int32), row, row), 5, 1, limit=60,
    )(counts, feat, cot, table, low, high)
    masked, grad, names, faces, picks, w_one, w_two = call(
        stage_kernel, "svvvvv",
        (flat, flat, ((rim, sites), F32), faces, picks, weight, weight), (), 1, 2,
    )(counts, feat, letters[1], letters[2], w_one, w_two)
    near, far = other_core(letters[0]), far_slab(letters[1])
    far_two, own_grad, hidden, mine, theirs = call(
        main_kernel, "svvvvvvvvv", (ends, field, flat, sums, sums),
        (broad, broad, ((WIDE, offsets * channels), BF)), 1, 5,
    )(counts, masked, grad, names, faces, picks, w_one, w_two, far, near)

    column, block = lax.axis_size(COLUMN), lax.axis_size(BLOCK)
    near = other_core(theirs)
    share = (mine.astype(F32) + near.astype(F32)).astype(BF)
    share, far_two = lax.optimization_barrier((share, far_two))
    parts = swap(share.reshape(block, -1, channels), BLOCK)
    far = far_slab(far_two)
    parts = (jnp.sum(parts.astype(F32), 0) * half).astype(BF)
    parts, far = lax.optimization_barrier((parts, far))
    parts = swap(jnp.broadcast_to(parts, (column, *parts.shape)), COLUMN)
    response, input_grad = call(
        last_kernel, "svvvvvvv", (flat, flat), (broad,), 1, 3
    )(counts, hidden, faces, near[offsets], far, own_grad, picks, w_two)
    total = (jnp.sum(parts.astype(F32), 0) * half).astype(BF)
    total, response, input_grad = lax.optimization_barrier((total, response, input_grad))

    whole = swap(jnp.broadcast_to(total, (block, *total.shape)), BLOCK)
    whole = whole.reshape(offsets + 1, channels, channels)
    other = other_core(whole)
    first_is_mine = lax.axis_index("core") == 0
    first = jnp.where(first_is_mine, whole, other)[:offsets]
    second = jnp.where(first_is_mine, other, whole)[:offsets]
    return response, input_grad, first, second


def solution(mesh):
    groups, slabs = mesh.devices.shape
    side = {64: 4, 16: 2, 4: 1}[slabs]
    pair = 2 if groups % 2 == 0 else 1
    fine = Mesh(mesh.devices.reshape(groups // pair, pair, side, side, 2, 2), AXES)
    rows, row = P(AXES, None), P(AXES)
    return jax.shard_map(
        on_device,
        mesh=fine,
        in_specs=(rows, row, rows, row, row, P(), P(), rows),
        out_specs=(rows, rows, P(), P()),
        check_vma=False,
    )
```
